128 devices in a mesh: seq: 32 (over x, y, core), fsdp: 4 (over z).
Axes of the slice: x: 4, y: 4, z: 4, core: 2. Of those that a mesh axis runs over, the one named last changes fastest.
Arguments:
- frames: bfloat16 [4, 6144, 1536], P('fsdp', 'seq'), may hold values from -6 to 6
- frame_mask: int32 [4, 6144], P('fsdp', 'seq'), may hold values from 0 to 1, as said below
- attend_gain: float32 [1536], replicated, may hold values from 0.25 to 1.75
- w_query: bfloat16 [1536, 1536], P(('seq', 'fsdp')), as said below
- w_key: bfloat16 [1536, 1536], P(('seq', 'fsdp')), as said below
- w_value: bfloat16 [1536, 1536], P(('seq', 'fsdp')), may hold values from -0.15625 to 0.15625
- w_out: bfloat16 [1536, 1536], P(('seq', 'fsdp')), may hold values from -0.15625 to 0.15625
- conv_gain: float32 [1536], replicated, may hold values from 0.25 to 1.75
- w_expand: bfloat16 [1536, 3072], P(('seq', 'fsdp')), may hold values from -0.15625 to 0.15625
- depth_kernel: float32 [31, 1536], replicated, may hold values from -1 to 1
- depth_gain: float32 [1536], replicated, may hold values from 0.25 to 1.75
- w_down: bfloat16 [1536, 1536], P(('seq', 'fsdp')), may hold values from -0.15625 to 0.15625
Outputs:
- block_out: bfloat16 [4, 6144, 1536], P('fsdp', 'seq')
The draws below stay inside these ranges and needn't reach their ends.
Inputs may be any that keep to these rules, and one draw needn't show every extreme that they name: `frame_mask`: in each utterance the real frames form a prefix of at least 3072 frames. `w_query`: independent zero-mean normal entries of one common spread. `w_key`: independent zero-mean normal entries of one common spread.
All inputs are finite; a program needn't handle non-finite values.
Results may differ from the reference program's by a relative error of at most 0.009.
The reference program's roundings to bfloat16 on the way count: a program that leaves them out, or rounds other values in their place, can miss the bound.
Values may be sent and summed in bfloat16 or wider, within the bound.
No kernel may reach another device: no remote copies, remote signals or barrier semaphores. Data moves between devices by JAX's collectives and lax.ppermute only.
A program may use at most 128 MiB of HBM per device.

```python
import math
import jax
import jax.numpy as jnp
from jax import lax

D = 1536
H = 16
HD = 96
KERNEL = 31
HALF = 15
FRAMES = 6144
UTTS = 4


def draw_frame_mask(key, part):
    key = jax.random.fold_in(key, 7)
    lengths = jax.random.randint(key, (UTTS,), FRAMES // 2, FRAMES + 1)
    return (jnp.arange(FRAMES)[None, :] < lengths[:, None]).astype(jnp.int32)


def draw_w_query(key, part):
    key = jax.random.fold_in(key, 11)
    values = jax.random.normal(key, (D, D), jnp.float32) * D ** (-0.5)
    return values.astype(jnp.bfloat16)


def draw_w_key(key, part):
    key = jax.random.fold_in(key, 13)
    values = jax.random.normal(key, (D, D), jnp.float32) * D ** (-0.5)
    return values.astype(jnp.bfloat16)


def steps_of(key, shape, pieces, low, top_value):
    def one(axis_at, shards_of):
        heights = jax.random.uniform(jax.random.fold_in(jax.random.fold_in(key, 6), axis_at), (shards_of,), jnp.float32, low / len(pieces), top_value / len(pieces))
        return jnp.repeat(jnp.exp(heights), shape[axis_at] // shards_of).reshape((-1,) + (1,) * (len(shape) - axis_at - 1))

    loudness = one(*pieces[0])
    for cut in pieces[1:]:
        loudness = loudness * one(*cut)
    return loudness


def scatter_about(stream_key, dims, scale, reach, pieces=(), held_as=jnp.bfloat16):
    level = steps_of(stream_key, dims, pieces, -0.22, 0.18) if pieces else 1.0
    values = jax.random.normal(stream_key, dims, jnp.float32) * scale * level
    return jnp.minimum(jnp.maximum(values, -reach), reach).astype(held_as)


def setup_inputs(seed: int = 0) -> dict:
    splits = jax.random.split(jax.random.key(seed), 13)
    frames = scatter_about(splits[0], (UTTS, FRAMES, D), 1.0, 6.0, ((0, 4), (1, 32)))
    frame_mask = draw_frame_mask(jax.random.fold_in(splits[12], 71), 0)
    attend_gain = jnp.clip(1.0 + 0.15 * jax.random.normal(splits[2], (D,), jnp.float32), 0.25, 1.75)
    w_query = draw_w_query(jax.random.fold_in(splits[12], 71), 0)
    w_key = draw_w_key(jax.random.fold_in(splits[12], 71), 0)
    w_value = scatter_about(splits[5], (D, D), D ** -0.5, 0.15625, ((0, 128),))
    w_out = scatter_about(splits[6], (D, D), D ** -0.5, 0.15625, ((0, 128),))
    conv_gain = jnp.clip(1.0 + 0.15 * jax.random.normal(splits[7], (D,), jnp.float32), 0.25, 1.75)
    w_expand = scatter_about(splits[8], (D, 2 * D), D ** -0.5, 0.15625, ((0, 128),))
    depth_kernel = scatter_about(splits[9], (KERNEL, D), KERNEL ** -0.5, 1.0, (), jnp.float32)
    depth_gain = jnp.clip(1.0 + 0.15 * jax.random.normal(splits[10], (D,), jnp.float32), 0.25, 1.75)
    w_down = scatter_about(splits[11], (D, D), D ** -0.5, 0.15625, ((0, 128),))
    return {"frames": frames, "frame_mask": frame_mask, "attend_gain": attend_gain, "w_query": w_query, "w_key": w_key, "w_value": w_value, "w_out": w_out, "conv_gain": conv_gain, "w_expand": w_expand, "depth_kernel": depth_kernel, "depth_gain": depth_gain, "w_down": w_down}


def layer_norm(values, gain):
    center = values - lax.optimization_barrier(jnp.mean(values, axis=-1, keepdims=True))
    spread = lax.optimization_barrier(jnp.mean(center * center, axis=-1, keepdims=True))
    return center * lax.rsqrt(spread + 1e-05) * gain

def attend(queries, key_rows, value_rows, mask_row):
    row_count = queries.shape[0]
    block = 512 if row_count % 512 == 0 else row_count
    allowed = mask_row > 0
    score_scale = 1.0 / math.sqrt(key_rows.shape[1])

    def one_block(block_rows):
        scores = jnp.dot(block_rows, key_rows.T, preferred_element_type=jnp.float32) * score_scale
        scores = jnp.where(allowed[None, :], scores, -1e+30)
        maxima = lax.optimization_barrier(jnp.max(scores, axis=1, keepdims=True))
        expos = jnp.exp(scores - maxima)
        probabilities = (expos / lax.optimization_barrier(jnp.sum(expos, axis=1, keepdims=True))).astype(jnp.bfloat16)
        return jnp.dot(probabilities, value_rows, preferred_element_type=jnp.float32).astype(jnp.bfloat16)
    outputs = lax.map(one_block, queries.reshape(row_count // block, block, queries.shape[1]))
    return outputs.reshape(row_count, value_rows.shape[1])

def split_heads(matrix):
    return matrix.reshape(UTTS, FRAMES, H, HD).transpose(0, 2, 1, 3).reshape(UTTS * H, FRAMES, HD)

def reference(frames, frame_mask, attend_gain, w_query, w_key, w_value, w_out, conv_gain, w_expand, depth_kernel, depth_gain, w_down):
    frames_wide = frames.astype(jnp.float32).reshape(UTTS * FRAMES, D)
    normed = layer_norm(frames_wide, attend_gain).astype(jnp.bfloat16)
    query_rows = jnp.dot(normed, w_query, preferred_element_type=jnp.float32).astype(jnp.bfloat16)
    key_rows = jnp.dot(normed, w_key, preferred_element_type=jnp.float32).astype(jnp.bfloat16)
    value_rows = jnp.dot(normed, w_value, preferred_element_type=jnp.float32).astype(jnp.bfloat16)
    head_masks = jnp.repeat(frame_mask, H, axis=0)
    attended = lax.map(lambda items: attend(items[0], items[1], items[2], items[3]), (split_heads(query_rows), split_heads(key_rows), split_heads(value_rows), head_masks))
    attended = attended.reshape(UTTS, H, FRAMES, HD).transpose(0, 2, 1, 3).reshape(UTTS * FRAMES, D)
    after_attend = frames_wide + jnp.dot(attended, w_out, preferred_element_type=jnp.float32)
    normed_conv = layer_norm(after_attend, conv_gain).astype(jnp.bfloat16)
    expanded = jnp.dot(normed_conv, w_expand, preferred_element_type=jnp.float32)
    mask_column = frame_mask.reshape(UTTS * FRAMES, 1).astype(jnp.float32)
    gated = (expanded[:, :D] * jax.nn.sigmoid(expanded[:, D:]) * mask_column).astype(jnp.bfloat16)
    padded = jnp.pad(gated.reshape(UTTS, FRAMES, D), ((0, 0), (HALF, HALF), (0, 0)))
    depthwise = jnp.zeros((UTTS, FRAMES, D), jnp.float32)
    for tap_index in range(KERNEL):
        depthwise = depthwise + padded[:, tap_index:tap_index + FRAMES].astype(jnp.float32) * depth_kernel[tap_index]
    activated = jax.nn.silu(layer_norm(depthwise, depth_gain)).astype(jnp.bfloat16).reshape(UTTS * FRAMES, D)
    block_out = after_attend + jnp.dot(activated, w_down, preferred_element_type=jnp.float32)
    return block_out.astype(jnp.bfloat16).reshape(UTTS, FRAMES, D)
```

```python
import functools
import math

import jax
import jax.numpy as jnp
from jax import lax
from jax.experimental import pallas as pl
from jax.experimental.pallas import tpu as pltpu
from jax.sharding import Mesh, PartitionSpec as P

D = 1536
ROWS = 192
HD = 96
HALF = 15
KERNEL = 31
SPLIT = 640
SLICE = 1152
BQ = 1024
BK = 256
SCALE = math.log2(math.e) / math.sqrt(HD)
NEG = -1e30
F32 = jnp.float32
BF16 = jnp.bfloat16
VMEM_LIMIT = 56 * 2**20


def pull(value, axis, step):
    count = lax.axis_size(axis)
    return lax.ppermute(value, axis, [((i + step) % count, i) for i in range(count)])


def gathered(value, axis):
    return [value] + [pull(value, axis, j) for j in (1, 2, 3)]


def to_absolute(pieces, own):
    twice = jnp.stack(pieces + pieces[:3])
    return lax.dynamic_slice_in_dim(twice, (4 - own) % 4, 4, 0)


def layer_norm(values, gain):
    center = values - jnp.mean(values, axis=-1, keepdims=True)
    spread = jnp.mean(center * center, axis=-1, keepdims=True)
    return center * lax.rsqrt(spread + 1e-05) * gain


def project_kernel(place, t0, t1, t2, t3, *rest):
    weights = rest[:16]
    q_out, kv_out, held, sems = rest[16:]
    x, y, c, z = place[0], place[1], place[2], place[3]
    copies = []
    for side in range(2):
        core = c if side == 0 else 1 - c
        for first in range(2):
            for outer in range(4):
                source = weights[side * 8 + first * 4 + outer]
                for inner in range(4):
                    if first == 0:
                        where = held.at[(x + inner) % 4, (y + outer) % 4, core, :, 0:SPLIT]
                    else:
                        where = held.at[(x + outer) % 4, (y + inner) % 4, core, :, SPLIT:SLICE]
                    copy = pltpu.make_async_copy(source.at[inner], where, sems.at[len(copies)])
                    copy.start()
                    copies.append(copy)
    for copy in copies:
        copy.wait()
    rows = jnp.concatenate([t0[...], t1[...], t2[...], t3[...]], axis=0)
    lane = lax.broadcasted_iota(jnp.int32, (ROWS, 128), 1)
    row = lax.broadcasted_iota(jnp.int32, (ROWS, 128), 0)
    for m in range(3):
        w = held[:, :, :, :, m * 384 : (m + 1) * 384].reshape(D, 384)
        product = jnp.dot(rows, w, preferred_element_type=F32)
        for j in range(4):
            u = (z + j) % 4
            for hh in range(4):
                part = product[j * ROWS : (j + 1) * ROWS, hh * HD : (hh + 1) * HD]
                part = jnp.concatenate([part, jnp.zeros((ROWS, 128 - HD), F32)], axis=1)
                if m == 1:
                    extra = jnp.where(row < place[4 + j], 0.0, NEG)
                else:
                    extra = jnp.ones((ROWS, 128), F32)
                part = jnp.where(lane == HD, extra, part).astype(BF16)
                if m == 0:
                    q_out[u * 4 + hh] = part
                else:
                    kv_out[u * 4 + hh, :, (m - 1) * 128 : m * 128] = part


def project(place, tokens, weights):
    vmem = pl.BlockSpec(memory_space=pltpu.VMEM)
    return pl.pallas_call(
        project_kernel,
        in_specs=[pl.BlockSpec(memory_space=pltpu.SMEM)]
        + [vmem] * 4
        + [pl.BlockSpec(memory_space=pl.ANY)] * 16,
        out_specs=(vmem, vmem),
        out_shape=(
            jax.ShapeDtypeStruct((16, ROWS, 128), BF16),
            jax.ShapeDtypeStruct((16, ROWS, 256), BF16),
        ),
        scratch_shapes=[
            pltpu.VMEM((4, 4, 2, 48, SLICE), BF16),
            pltpu.SemaphoreType.DMA((64,)),
        ],
        compiler_params=pltpu.CompilerParams(vmem_limit_bytes=VMEM_LIMIT),
        cost_estimate=pl.CostEstimate(
            flops=2 * 768 * D * SLICE, bytes_accessed=12 * 2**20, transcendentals=0
        ),
        name="project",
    )(place, *tokens, *weights)


def attend_kernel(q_ref, own_ref, other_ref, o_ref, norm_ref):
    total = own_ref.shape[0]
    steps = total // BK

    def largest(rows):
        wide = rows[:, 0:HD].astype(F32)
        return jnp.max(jnp.sum(wide * wide, axis=1, keepdims=True))

    @pl.when(pl.program_id(0) == 0)
    def _():
        norm_ref[0] = jnp.maximum(largest(own_ref[:, 0:128]), largest(other_ref[:, 0:128]))

    q = q_ref[...]
    bounded = largest(q) * norm_ref[0] <= 60.0 * 60.0 * HD

    def scores(ref, start):
        return lax.dot_general(
            q,
            ref[pl.ds(start, BK), 0:128],
            (((1,), (1,)), ((), ())),
            preferred_element_type=F32,
        )

    def finish(acc):
        o_ref[...] = (acc * (1.0 / acc[:, HD : HD + 1])).astype(BF16)

    @pl.when(bounded)
    def _():
        acc = jnp.zeros((q.shape[0], 128), F32)
        for i in range(steps):
            for ref in (own_ref, other_ref):
                p = jnp.exp2(scores(ref, i * BK) * SCALE).astype(BF16)
                acc = acc + jnp.dot(
                    p, ref[pl.ds(i * BK, BK), 128:256], preferred_element_type=F32
                )
        finish(acc)

    @pl.when(jnp.logical_not(bounded))
    def _():
        def body(i, carry):
            peak, acc = carry
            start = pl.multiple_of(i * BK, BK)
            for ref in (own_ref, other_ref):
                s = scores(ref, start) * SCALE
                higher = jnp.maximum(peak, jnp.max(s, axis=1, keepdims=True))
                p = jnp.exp2(s - higher).astype(BF16)
                acc = acc * jnp.exp2(peak - higher) + jnp.dot(
                    p, ref[pl.ds(start, BK), 128:256], preferred_element_type=F32
                )
                peak = higher
            return peak, acc

        start = (
            jnp.full((q.shape[0], 1), -3e38, F32),
            jnp.zeros((q.shape[0], 128), F32),
        )
        finish(lax.fori_loop(0, steps, body, start)[1])


def attend(q, own, other):
    total = q.shape[0]
    whole = pl.BlockSpec((total, 256), lambda i: (0, 0))
    return pl.pallas_call(
        attend_kernel,
        grid=(total // BQ,),
        in_specs=[pl.BlockSpec((BQ, 128), lambda i: (i, 0)), whole, whole],
        out_specs=pl.BlockSpec((BQ, 128), lambda i: (i, 0)),
        out_shape=jax.ShapeDtypeStruct((total, 128), BF16),
        scratch_shapes=[pltpu.SMEM((1,), F32)],
        compiler_params=pltpu.CompilerParams(vmem_limit_bytes=VMEM_LIMIT),
        cost_estimate=pl.CostEstimate(
            flops=4 * total * total * 2 * 256, bytes_accessed=5 * 2**20, transcendentals=0
        ),
        name="attend",
    )(q, own, other)


def expand_kernel(count, att, frames, gain, weights, after_out, gated_out, rows, held, sems):
    copies = [
        pltpu.make_async_copy(weights.at[:, k], held.at[k], sems.at[k]) for k in range(3)
    ]
    for copy in copies:
        copy.start()
    for h in range(16):
        rows[:, h * HD : (h + 1) * HD] = att[h, :, 0:HD]
    copies[0].wait()
    out_term = jnp.dot(rows[...], held[0].reshape(D, D), preferred_element_type=F32)
    after = frames[...].astype(F32) + out_term
    after_out[...] = after
    normed = layer_norm(after, gain[...]).astype(BF16)
    copies[1].wait()
    copies[2].wait()
    real = lax.broadcasted_iota(jnp.int32, (ROWS, 1), 0) < count[0]
    for n in range(3):
        cols = slice(n * 512, (n + 1) * 512)
        left = jnp.dot(normed, held[1, :, :, cols].reshape(D, 512), preferred_element_type=F32)
        right = jnp.dot(normed, held[2, :, :, cols].reshape(D, 512), preferred_element_type=F32)
        gate = left * (1.0 / (1.0 + jnp.exp(-right)))
        gated_out[:, cols] = jnp.where(real, gate, 0.0).astype(BF16)


def expand(count, att, frames, gain, weights):
    vmem = pl.BlockSpec(memory_space=pltpu.VMEM)
    return pl.pallas_call(
        expand_kernel,
        in_specs=[
            pl.BlockSpec(memory_space=pltpu.SMEM),
            vmem,
            vmem,
            vmem,
            pl.BlockSpec(memory_space=pl.ANY),
        ],
        out_specs=(vmem, vmem),
        out_shape=(
            jax.ShapeDtypeStruct((ROWS, D), F32),
            jax.ShapeDtypeStruct((ROWS, D), BF16),
        ),
        scratch_shapes=[
            pltpu.VMEM((ROWS, D), BF16),
            pltpu.VMEM((3, 32, 48, D), BF16),
            pltpu.SemaphoreType.DMA((3,)),
        ],
        compiler_params=pltpu.CompilerParams(vmem_limit_bytes=VMEM_LIMIT),
        cost_estimate=pl.CostEstimate(
            flops=2 * ROWS * D * D * 3, bytes_accessed=16 * 2**20, transcendentals=ROWS * D
        ),
        name="expand",
    )(count, att, frames, gain, weights)


def down_kernel(gated, before, behind, after, taps, gain, weights, out, wide, mixed, held, sem):
    copy = pltpu.make_async_copy(weights.at[:, 3], held, sem)
    copy.start()
    wide[0:16, :] = before[...].astype(F32)
    wide[16 : 16 + ROWS, :] = gated[...].astype(F32)
    wide[16 + ROWS : 32 + ROWS, :] = behind[...].astype(F32)
    for n in range(D // 128):
        cols = slice(n * 128, (n + 1) * 128)
        acc = jnp.zeros((ROWS, 128), F32)
        for s in range(8):
            length = ROWS + 8 * ((KERNEL - s) // 8)
            shifted = wide[s : s + length, cols]
            for a in range(4):
                k = 8 * a + s - 1
                if 0 <= k < KERNEL:
                    acc = acc + shifted[8 * a : 8 * a + ROWS] * taps[k : k + 1, cols]
        mixed[:, cols] = acc
    normed = layer_norm(mixed[...], gain[...])
    activated = (normed / (1.0 + jnp.exp(-normed))).astype(BF16)
    copy.wait()
    down = jnp.dot(activated, held[...].reshape(D, D), preferred_element_type=F32)
    out[...] = (after[...] + down).astype(BF16)


def down(gated, before, behind, after, taps, gain, weights):
    vmem = pl.BlockSpec(memory_space=pltpu.VMEM)
    return pl.pallas_call(
        down_kernel,
        in_specs=[vmem] * 6 + [pl.BlockSpec(memory_space=pl.ANY)],
        out_specs=vmem,
        out_shape=jax.ShapeDtypeStruct((ROWS, D), BF16),
        scratch_shapes=[
            pltpu.VMEM((ROWS + 32, D), F32),
            pltpu.VMEM((ROWS, D), F32),
            pltpu.VMEM((32, 48, D), BF16),
            pltpu.SemaphoreType.DMA,
        ],
        compiler_params=pltpu.CompilerParams(vmem_limit_bytes=VMEM_LIMIT),
        cost_estimate=pl.CostEstimate(
            flops=2 * ROWS * D * D, bytes_accessed=8 * 2**20, transcendentals=ROWS * D
        ),
        name="down",
    )(gated, before, behind, after, taps, gain, weights)


def on_device(
    frames,
    frame_mask,
    attend_gain,
    w_query,
    w_key,
    w_value,
    w_out,
    conv_gain,
    w_expand,
    depth_kernel,
    depth_gain,
    w_down,
):
    x, y, c, z = (lax.axis_index(a) for a in ("x", "y", "c", "z"))
    own_frames = frames[0]

    slices = jnp.stack(
        [w.reshape(12, 4, 384) for w in (w_query, w_key, w_value)], axis=2
    ).transpose(1, 0, 2, 3).reshape(4, 12, SLICE)
    pieces = [
        pull(lax.dynamic_index_in_dim(slices, (z - j) % 4, 0, keepdims=False), "z", j) if j
        else lax.dynamic_index_in_dim(slices, z, 0, keepdims=False)
        for j in range(4)
    ]
    rows48 = to_absolute(pieces, z).reshape(48, SLICE)

    others = jnp.stack([w_out, w_expand[:, :D], w_expand[:, D:], w_down])
    others = to_absolute(gathered(others, "z"), z).transpose(1, 0, 2, 3).reshape(4, 48, D)
    weights = lax.all_gather(others, ("x", "y", "c"), axis=0)

    normed = layer_norm(own_frames.astype(F32), attend_gain).astype(BF16)
    tokens = gathered(normed, "z")
    own_count = jnp.sum(frame_mask[0])
    counts = gathered(jnp.full((8, 128), own_count, jnp.int32), "z")
    place = jnp.stack([x, y, c, z] + [count[0, 0] for count in counts]).astype(jnp.int32)

    first, second = rows48[:, :SPLIT], rows48[:, SPLIT:]
    first = gathered(jnp.stack(gathered(first, "x")), "y")
    second = gathered(jnp.stack(gathered(second, "y")), "x")
    mine = first + second
    theirs = [pull(piece, "c", 1) for piece in mine]
    q, kv = project(place, tokens, mine + theirs)

    kv = lax.all_to_all(kv, ("x", "y"), split_axis=0, concat_axis=0, tiled=True)
    kv = kv.reshape(16 * ROWS, 256)
    kv_other = pull(kv, "c", 1)
    q = lax.all_to_all(q, ("x", "y"), split_axis=0, concat_axis=0, tiled=True)
    attended = attend(q.reshape(16 * ROWS, 128), kv, kv_other)

    swap = [(a * 4 + b, b * 4 + a) for a in range(4) for b in range(4)]
    attended = lax.ppermute(attended.reshape(16, ROWS, 128), ("x", "z"), swap)
    attended = lax.all_to_all(attended, ("x", "y"), split_axis=0, concat_axis=0, tiled=True)

    after, gated = expand(
        own_count.reshape(1).astype(jnp.int32), attended, own_frames, conv_gain[None], weights
    )
    line = ("x", "y", "c")
    before = lax.ppermute(gated[ROWS - 16 :], line, [(i, i + 1) for i in range(31)])
    behind = lax.ppermute(gated[:16], line, [(i + 1, i) for i in range(31)])
    return down(gated, before, behind, after, depth_kernel, depth_gain[None], weights)[None]


def solution(mesh):
    cells = Mesh(mesh.devices.reshape(4, 4, 2, 4), ("x", "y", "c", "z"))
    seq = ("x", "y", "c")
    spread = P(("x", "y", "c", "z"), None)
    in_specs = (
        P("z", seq, None),
        P("z", seq),
        P(),
        spread,
        spread,
        spread,
        spread,
        P(),
        spread,
        P(),
        P(),
        spread,
    )
    return jax.shard_map(
        on_device, mesh=cells, in_specs=in_specs, out_specs=P("z", seq, None), check_vma=False
    )
```

```python
import functools
import math

import jax
import jax.numpy as jnp
from jax import lax
from jax.experimental import pallas as pl
from jax.experimental.pallas import tpu as pltpu
from jax.sharding import Mesh, PartitionSpec as P

D = 1536
ROWS = 192
HD = 96
HALF = 15
KERNEL = 31
PART = 96
PIECES = ((0, 0), (1, 0), (3, 0), (2, 0), (2, 2))
BQ = 1024
BK = 256
SCALE = math.log2(math.e) / math.sqrt(HD)
NEG = -1e30
F32 = jnp.float32
BF16 = jnp.bfloat16
VMEM_LIMIT = 56 * 2**20


def pull(value, axis, step):
    count = lax.axis_size(axis)
    return lax.ppermute(value, axis, [((i + step) % count, i) for i in range(count)])


def gathered(value, axis):
    return [value] + [pull(value, axis, j) for j in (1, 2, 3)]


def exchanged(blocks, own, axis):
    pieces = [lax.dynamic_index_in_dim(blocks, (own - j) % 4, 0, keepdims=False) for j in range(4)]
    return pieces[:1] + [pull(pieces[j], axis, j) for j in (1, 2, 3)]


def plane(rows, inner, outer):
    line = jnp.stack(gathered(rows, inner))
    after, before = pull(line, outer, 1), pull(line, outer, 3)
    return [line, after, before, pull(after[:2], outer, 1), pull(before[2:], outer, 3)]


def to_absolute(pieces, own):
    twice = jnp.stack(pieces + pieces[:3])
    return lax.dynamic_slice_in_dim(twice, (4 - own) % 4, 4, 0)


def layer_norm(values, gain):
    center = values - jnp.mean(values, axis=-1, keepdims=True)
    spread = jnp.mean(center * center, axis=-1, keepdims=True)
    return center * lax.rsqrt(spread + 1e-05) * gain


def project_kernel(place, *refs):
    pieces, (own_w, other_w, q_out, kv_out, rows, held, sems, w_sems) = refs[:10], refs[10:]
    x, y, c = place[0], place[1], place[2]
    w_copies = [
        pltpu.make_async_copy(own_w, held.at[:, c], w_sems.at[0]),
        pltpu.make_async_copy(other_w, held.at[:, 1 - c], w_sems.at[1]),
    ]
    for copy in w_copies:
        copy.start()
    copies, start = [], 0
    for p, piece in enumerate(pieces):
        n = piece.shape[0]
        copies.append(pltpu.make_async_copy(piece, rows.at[pl.ds(start, n)], sems.at[p]))
        copies[-1].start()
        start += n
    for copy in w_copies:
        copy.wait()
    w = held[...].reshape(D, 384)
    lane = lax.broadcasted_iota(jnp.int32, (PART, 128), 1)
    row = lax.broadcasted_iota(jnp.int32, (PART, 128), 0)
    start = 0
    for p, piece in enumerate(pieces):
        n = piece.shape[0]
        side, (outer, inner) = p // 5, PIECES[p % 5]
        copies[p].wait()
        product = jnp.dot(
            rows[start : start + n].reshape(n * PART, D), w, preferred_element_type=F32
        )
        start += n
        for j in range(n):
            if side == 0:
                chunk = (x + inner + j) % 4 * 4 + (y + outer) % 4
            else:
                chunk = (x + outer) % 4 * 4 + (y + inner + j) % 4
            first = side * PART
            part = product[j * PART : (j + 1) * PART]
            bias = jnp.where(row + first < place[4 + chunk], 0.0, NEG)
            span = pl.ds(first, PART)
            q_out[chunk, span, :] = jnp.where(lane == HD, 1.0, part[:, 0:128]).astype(BF16)
            kv_out[chunk, span, 0:128] = jnp.where(lane == HD, bias, part[:, 128:256]).astype(BF16)
            kv_out[chunk, span, 128:256] = jnp.where(lane == HD, 1.0, part[:, 256:384]).astype(BF16)


def project(place, pieces, own_w, other_w):
    vmem = pl.BlockSpec(memory_space=pltpu.VMEM)
    return pl.pallas_call(
        project_kernel,
        in_specs=[pl.BlockSpec(memory_space=pltpu.SMEM)]
        + [pl.BlockSpec(memory_space=pl.ANY)] * 12,
        out_specs=(vmem, vmem),
        out_shape=(
            jax.ShapeDtypeStruct((16, ROWS, 128), BF16),
            jax.ShapeDtypeStruct((16, ROWS, 256), BF16),
        ),
        scratch_shapes=[
            pltpu.VMEM((32, PART, D), BF16),
            pltpu.VMEM((16, 2, 48, 384), BF16),
            pltpu.SemaphoreType.DMA((10,)),
            pltpu.SemaphoreType.DMA((2,)),
        ],
        compiler_params=pltpu.CompilerParams(vmem_limit_bytes=VMEM_LIMIT),
        cost_estimate=pl.CostEstimate(
            flops=2 * 3072 * D * 384, bytes_accessed=13 * 2**20, transcendentals=0
        ),
        name="project",
    )(place, *pieces, own_w, other_w)


def attend_kernel(q_ref, own_ref, other_ref, o_ref, norm_ref):
    total = own_ref.shape[0]
    steps = total // BK

    def largest(rows):
        wide = rows[:, 0:HD].astype(F32)
        return jnp.max(jnp.sum(wide * wide, axis=1, keepdims=True))

    @pl.when(pl.program_id(0) == 0)
    def _():
        norm_ref[0] = jnp.maximum(largest(own_ref[:, 0:128]), largest(other_ref[:, 0:128]))

    q = q_ref[...]
    bounded = largest(q) * norm_ref[0] <= 60.0 * 60.0 * HD

    def scores(ref, start):
        return lax.dot_general(
            q,
            ref[pl.ds(start, BK), 0:128],
            (((1,), (1,)), ((), ())),
            preferred_element_type=F32,
        )

    def finish(acc):
        o_ref[...] = (acc * (1.0 / acc[:, HD : HD + 1])).astype(BF16)

    @pl.when(bounded)
    def _():
        acc = jnp.zeros((q.shape[0], 128), F32)
        for i in range(steps):
            for ref in (own_ref, other_ref):
                p = jnp.exp2(scores(ref, i * BK) * SCALE).astype(BF16)
                acc = acc + jnp.dot(
                    p, ref[pl.ds(i * BK, BK), 128:256], preferred_element_type=F32
                )
        finish(acc)

    @pl.when(jnp.logical_not(bounded))
    def _():
        def body(i, carry):
            peak, acc = carry
            start = pl.multiple_of(i * BK, BK)
            for ref in (own_ref, other_ref):
                s = scores(ref, start) * SCALE
                higher = jnp.maximum(peak, jnp.max(s, axis=1, keepdims=True))
                p = jnp.exp2(s - higher).astype(BF16)
                acc = acc * jnp.exp2(peak - higher) + jnp.dot(
                    p, ref[pl.ds(start, BK), 128:256], preferred_element_type=F32
                )
                peak = higher
            return peak, acc

        start = (
            jnp.full((q.shape[0], 1), -3e38, F32),
            jnp.zeros((q.shape[0], 128), F32),
        )
        finish(lax.fori_loop(0, steps, body, start)[1])


def attend(q, own, other):
    total = q.shape[0]
    whole = pl.BlockSpec((total, 256), lambda i: (0, 0))
    return pl.pallas_call(
        attend_kernel,
        grid=(total // BQ,),
        in_specs=[pl.BlockSpec((BQ, 128), lambda i: (i, 0)), whole, whole],
        out_specs=pl.BlockSpec((BQ, 128), lambda i: (i, 0)),
        out_shape=jax.ShapeDtypeStruct((total, 128), BF16),
        scratch_shapes=[pltpu.SMEM((1,), F32)],
        compiler_params=pltpu.CompilerParams(vmem_limit_bytes=VMEM_LIMIT),
        cost_estimate=pl.CostEstimate(
            flops=4 * total * total * 2 * 256, bytes_accessed=5 * 2**20, transcendentals=0
        ),
        name="attend",
    )(q, own, other)


def expand_kernel(count, att, frames, gain, weights, after_out, gated_out, rows, held, sems):
    copies = [
        pltpu.make_async_copy(weights.at[:, k], held.at[k], sems.at[k]) for k in range(3)
    ]
    for copy in copies:
        copy.start()
    for h in range(16):
        rows[:, h * HD : (h + 1) * HD] = att[h, :, 0:HD]
    copies[0].wait()
    out_term = jnp.dot(rows[...], held[0].reshape(D, D), preferred_element_type=F32)
    after = frames[...].astype(F32) + out_term
    after_out[...] = after
    normed = layer_norm(after, gain[...]).astype(BF16)
    copies[1].wait()
    copies[2].wait()
    real = lax.broadcasted_iota(jnp.int32, (ROWS, 1), 0) < count[0]
    for n in range(3):
        cols = slice(n * 512, (n + 1) * 512)
        left = jnp.dot(normed, held[1, :, :, cols].reshape(D, 512), preferred_element_type=F32)
        right = jnp.dot(normed, held[2, :, :, cols].reshape(D, 512), preferred_element_type=F32)
        gate = left * (1.0 / (1.0 + jnp.exp(-right)))
        gated_out[:, cols] = jnp.where(real, gate, 0.0).astype(BF16)


def expand(count, att, frames, gain, weights):
    vmem = pl.BlockSpec(memory_space=pltpu.VMEM)
    return pl.pallas_call(
        expand_kernel,
        in_specs=[
            pl.BlockSpec(memory_space=pltpu.SMEM),
            vmem,
            vmem,
            vmem,
            pl.BlockSpec(memory_space=pl.ANY),
        ],
        out_specs=(vmem, vmem),
        out_shape=(
            jax.ShapeDtypeStruct((ROWS, D), F32),
            jax.ShapeDtypeStruct((ROWS, D), BF16),
        ),
        scratch_shapes=[
            pltpu.VMEM((ROWS, D), BF16),
            pltpu.VMEM((3, 32, 48, D), BF16),
            pltpu.SemaphoreType.DMA((3,)),
        ],
        compiler_params=pltpu.CompilerParams(vmem_limit_bytes=VMEM_LIMIT),
        cost_estimate=pl.CostEstimate(
            flops=2 * ROWS * D * D * 3, bytes_accessed=16 * 2**20, transcendentals=ROWS * D
        ),
        name="expand",
    )(count, att, frames, gain, weights)


def down_kernel(gated, before, behind, after, taps, gain, weights, out, wide, mixed, held, sem):
    copy = pltpu.make_async_copy(weights.at[:, 3], held, sem)
    copy.start()
    wide[0:16, :] = before[...].astype(F32)
    wide[16 : 16 + ROWS, :] = gated[...].astype(F32)
    wide[16 + ROWS : 32 + ROWS, :] = behind[...].astype(F32)
    for n in range(D // 128):
        cols = slice(n * 128, (n + 1) * 128)
        acc = jnp.zeros((ROWS, 128), F32)
        for s in range(8):
            length = ROWS + 8 * ((KERNEL - s) // 8)
            shifted = wide[s : s + length, cols]
            for a in range(4):
                k = 8 * a + s - 1
                if 0 <= k < KERNEL:
                    acc = acc + shifted[8 * a : 8 * a + ROWS] * taps[k : k + 1, cols]
        mixed[:, cols] = acc
    normed = layer_norm(mixed[...], gain[...])
    activated = (normed / (1.0 + jnp.exp(-normed))).astype(BF16)
    copy.wait()
    down = jnp.dot(activated, held[...].reshape(D, D), preferred_element_type=F32)
    out[...] = (after[...] + down).astype(BF16)


def down(gated, before, behind, after, taps, gain, weights):
    vmem = pl.BlockSpec(memory_space=pltpu.VMEM)
    return pl.pallas_call(
        down_kernel,
        in_specs=[vmem] * 6 + [pl.BlockSpec(memory_space=pl.ANY)],
        out_specs=vmem,
        out_shape=jax.ShapeDtypeStruct((ROWS, D), BF16),
        scratch_shapes=[
            pltpu.VMEM((ROWS + 32, D), F32),
            pltpu.VMEM((ROWS, D), F32),
            pltpu.VMEM((32, 48, D), BF16),
            pltpu.SemaphoreType.DMA,
        ],
        compiler_params=pltpu.CompilerParams(vmem_limit_bytes=VMEM_LIMIT),
        cost_estimate=pl.CostEstimate(
            flops=2 * ROWS * D * D, bytes_accessed=8 * 2**20, transcendentals=ROWS * D
        ),
        name="down",
    )(gated, before, behind, after, taps, gain, weights)


def on_device(
    frames,
    frame_mask,
    attend_gain,
    w_query,
    w_key,
    w_value,
    w_out,
    conv_gain,
    w_expand,
    depth_kernel,
    depth_gain,
    w_down,
):
    x, y, c, z = (lax.axis_index(a) for a in ("x", "y", "c", "z"))
    own_frames = frames[0]

    others = jnp.stack([w_out, w_expand[:, :D], w_expand[:, D:], w_down])
    others = to_absolute(exchanged(others, z, "z"), z).reshape(48, D)
    weights = lax.all_gather(others, ("x", "y", "c", "z"), axis=0).reshape(32, 4, 48, D)

    normed = layer_norm(own_frames.astype(F32), attend_gain).astype(BF16)
    pieces = plane(normed[:PART], "x", "y") + plane(normed[PART:], "y", "x")

    own_count = jnp.sum(frame_mask[0])
    heads = jnp.stack([w.reshape(12, 16, HD) for w in (w_query, w_key, w_value)], axis=2)
    heads = jnp.pad(heads, ((0, 0), (0, 0), (0, 0), (0, 128 - HD)))
    heads = heads.reshape(12, 16, 384).transpose(1, 0, 2)
    at_count = (jnp.arange(384) == HD)[None, None, :]
    heads = jnp.where(at_count, own_count.astype(BF16), heads)
    heads = lax.all_to_all(heads, ("x", "y"), split_axis=0, concat_axis=0, tiled=True)
    counts = heads[:, 0, HD].astype(jnp.int32)
    own_w = to_absolute(gathered(heads, "z"), z).transpose(1, 0, 2, 3).reshape(16, 48, 384)
    other_w = pull(own_w, "c", 1)
    place = jnp.concatenate([jnp.stack([x, y, c, z]).astype(jnp.int32), counts])

    q, kv = project(place, pieces, own_w, other_w)
    kv = kv.reshape(16 * ROWS, 256)
    attended = attend(q.reshape(16 * ROWS, 128), kv, pull(kv, "c", 1))
    attended = attended.reshape(16, ROWS, 128)
    attended = lax.all_to_all(attended, ("x", "y"), split_axis=0, concat_axis=0, tiled=True)

    after, gated = expand(
        own_count.reshape(1).astype(jnp.int32), attended, own_frames, conv_gain[None], weights
    )
    line = ("x", "y", "c")
    before = lax.ppermute(gated[ROWS - 16 :], line, [(i, i + 1) for i in range(31)])
    behind = lax.ppermute(gated[:16], line, [(i + 1, i) for i in range(31)])
    return down(gated, before, behind, after, depth_kernel, depth_gain[None], weights)[None]


def solution(mesh):
    cells = Mesh(mesh.devices.reshape(4, 4, 2, 4), ("x", "y", "c", "z"))
    seq = ("x", "y", "c")
    spread = P(("x", "y", "c", "z"), None)
    in_specs = (
        P("z", seq, None),
        P("z", seq),
        P(),
        spread,
        spread,
        spread,
        spread,
        P(),
        spread,
        P(),
        P(),
        spread,
    )
    return jax.shard_map(
        on_device, mesh=cells, in_specs=in_specs, out_specs=P("z", seq, None), check_vma=False
    )
```

```python
import functools
import math

import jax
import jax.numpy as jnp
from jax import lax
from jax.experimental import pallas as pl
from jax.experimental.pallas import tpu as pltpu
from jax.sharding import Mesh, PartitionSpec as P

D = 1536
ROWS = 192
HD = 96
KERNEL = 31
PART = 96
EARLY = 24 * PART
LATE = 8 * PART
BQ = LATE
BK = 256
SCALE = math.log2(math.e) / math.sqrt(HD)
NEG = -1e30
F32 = jnp.float32
BF16 = jnp.bfloat16
VMEM_LIMIT = 56 * 2**20
VMEM = pl.BlockSpec(memory_space=pltpu.VMEM)
SMEM = pl.BlockSpec(memory_space=pltpu.SMEM)
HBM = pl.BlockSpec(memory_space=pl.ANY)
PARAMS = pltpu.CompilerParams(vmem_limit_bytes=VMEM_LIMIT)


def pull(value, axis, step):
    count = lax.axis_size(axis)
    return lax.ppermute(value, axis, [((i + step) % count, i) for i in range(count)])


def gathered(value, axis):
    return [value] + [pull(value, axis, j) for j in (1, 2, 3)]


def plane(line, outer):
    after, before = pull(line, outer, 1), pull(line, outer, 3)
    return [line, after, before], [pull(after[:2], outer, 1), pull(before[2:], outer, 3)]


def order(x, y):
    chunks, sides = [], []
    for side in range(2):
        for outer in (0, 1, 3):
            for inner in range(4):
                chunks.append((outer, inner))
                sides.append(side)
    for side in range(2):
        for inner in range(4):
            chunks.append((2, inner))
            sides.append(side)
    outer = jnp.array([o for o, _ in chunks], jnp.int32)
    inner = jnp.array([i for _, i in chunks], jnp.int32)
    side = jnp.array(sides, jnp.int32)
    across = jnp.where(side == 0, inner, outer)
    along = jnp.where(side == 0, outer, inner)
    return (x + across) % 4 * 4 + (y + along) % 4, side


def layer_norm(values, gain):
    center = values - jnp.mean(values, axis=-1, keepdims=True)
    spread = jnp.mean(center * center, axis=-1, keepdims=True)
    return center * lax.rsqrt(spread + 1e-05) * gain


def project_rows(first, counts, rows, w, q_out, kv_out):
    n = rows.shape[0]
    lane = lax.broadcasted_iota(jnp.int32, (PART, 128), 1)
    row = lax.broadcasted_iota(jnp.int32, (PART, 128), 0)
    product = jnp.dot(rows.reshape(n * PART, D), w, preferred_element_type=F32)
    for j in range(n):
        part = product[j * PART : (j + 1) * PART]
        bias = jnp.where(row < counts[first + j], 0.0, NEG)
        span = slice((first + j) % 24 * PART, ((first + j) % 24 + 1) * PART)
        q_out[span, :] = jnp.where(lane == HD, 1.0, part[:, 0:128]).astype(BF16)
        kv_out[span, 0:128] = jnp.where(lane == HD, bias, part[:, 128:256]).astype(BF16)
        kv_out[span, 128:256] = jnp.where(lane == HD, 1.0, part[:, 256:384]).astype(BF16)


def early_kernel(place, counts, *refs):
    pieces, (own_w, other_w, q_out, kv_out, w_out, rows, held, sems) = refs[:6], refs[6:]
    c, z = place[0], place[1]
    w_copies, copies = [], []
    for side, source in enumerate((own_w, other_w)):
        core = c if side == 0 else 1 - c
        for j in range(4):
            w_copies.append(
                pltpu.make_async_copy(
                    source.at[j], held.at[core, (z + j) % 4], sems.at[6 + side * 4 + j]
                )
            )
            w_copies[-1].start()
    for p in range(6):
        copies.append(
            pltpu.make_async_copy(pieces[p], rows.at[4 * p : 4 * p + 4], sems.at[p])
        )
        copies[-1].start()
    for copy in w_copies:
        copy.wait()
    for chunk in range(16):
        for core in range(2):
            w_out[(chunk * 2 + core) * 48 : (chunk * 2 + core + 1) * 48, :] = jnp.concatenate(
                [held[core, k, chunk, 0:12, :] for k in range(4)], axis=0
            )
    for side in range(2):
        for p in range(3):
            copies[side * 3 + p].wait()
        project_rows(
            12 * side, counts, rows[12 * side : 12 * side + 12], w_out[...], q_out, kv_out
        )


def project_early(place, counts, pieces, own_w, other_w):
    return pl.pallas_call(
        early_kernel,
        in_specs=[SMEM, SMEM] + [HBM] * 8,
        out_specs=(VMEM, VMEM, VMEM),
        out_shape=(
            jax.ShapeDtypeStruct((EARLY, 128), BF16),
            jax.ShapeDtypeStruct((EARLY, 256), BF16),
            jax.ShapeDtypeStruct((D, 384), BF16),
        ),
        scratch_shapes=[
            pltpu.VMEM((24, PART, D), BF16),
            pltpu.VMEM((2, 4, 16, 16, 384), BF16),
            pltpu.SemaphoreType.DMA((14,)),
        ],
        compiler_params=PARAMS,
        cost_estimate=pl.CostEstimate(
            flops=EARLY * D * 128, bytes_accessed=2**20, transcendentals=0
        ),
        name="project_early",
    )(place, counts, *pieces, own_w, other_w)


def late_kernel(counts, p0, p1, p2, p3, w, q_out, kv_out, rows, sems):
    copies = [
        pltpu.make_async_copy(p, rows.at[2 * i : 2 * i + 2], sems.at[i])
        for i, p in enumerate((p0, p1, p2, p3))
    ]
    for copy in copies:
        copy.start()
    for copy in copies:
        copy.wait()
    project_rows(24, counts, rows[...], w[...], q_out, kv_out)


def project_late(counts, pieces, w):
    return pl.pallas_call(
        late_kernel,
        in_specs=[SMEM] + [HBM] * 4 + [VMEM],
        out_specs=(VMEM, VMEM),
        out_shape=(
            jax.ShapeDtypeStruct((LATE, 128), BF16),
            jax.ShapeDtypeStruct((LATE, 256), BF16),
        ),
        scratch_shapes=[pltpu.VMEM((8, PART, D), BF16), pltpu.SemaphoreType.DMA((4,))],
        compiler_params=PARAMS,
        cost_estimate=pl.CostEstimate(
            flops=2 * LATE * D * 512, bytes_accessed=4 * 2**20, transcendentals=0
        ),
        name="project_late",
    )(counts, *pieces, w)


def largest(rows):
    wide = rows[:, 0:HD].astype(F32)
    return jnp.max(jnp.sum(wide * wide, axis=1, keepdims=True))


def attend_block(q, sources, bounded, first, finish):
    def scores(ref, start):
        return lax.dot_general(
            q,
            ref[pl.ds(start, BK), 0:128],
            (((1,), (1,)), ((), ())),
            preferred_element_type=F32,
        )

    def start_values():
        if first is None:
            return jnp.full((BQ, 1), -3e38, F32), jnp.zeros((BQ, 128), F32)
        return first()

    @pl.when(bounded)
    def _():
        acc = start_values()[1]
        for ref in sources:
            for i in range(ref.shape[0] // BK):
                p = jnp.exp2(scores(ref, i * BK) * SCALE).astype(BF16)
                acc = acc + jnp.dot(
                    p, ref[pl.ds(i * BK, BK), 128:256], preferred_element_type=F32
                )
        finish(jnp.zeros((BQ, 1), F32), acc)

    @pl.when(jnp.logical_not(bounded))
    def _():
        def body(ref, i, carry):
            peak, acc = carry
            start = pl.multiple_of(i * BK, BK)
            s = scores(ref, start) * SCALE
            higher = jnp.maximum(peak, jnp.max(s, axis=1, keepdims=True))
            p = jnp.exp2(s - higher).astype(BF16)
            acc = acc * jnp.exp2(peak - higher) + jnp.dot(
                p, ref[pl.ds(start, BK), 128:256], preferred_element_type=F32
            )
            return higher, acc

        carry = start_values()
        for ref in sources:
            carry = lax.fori_loop(
                0, ref.shape[0] // BK, functools.partial(body, ref), carry
            )
        finish(*carry)


def limit(q, norm):
    return largest(q) * norm <= 60.0 * 60.0 * HD


def attend_early_kernel(q_ref, own, other, o_ref, norm):
    @pl.when(pl.program_id(0) == 0)
    def _():
        norm[0] = jnp.maximum(largest(own[:, 0:128]), largest(other[:, 0:128]))

    def finish(shift, acc):
        lane = lax.broadcasted_iota(jnp.int32, (BQ, 128), 1)
        acc = jnp.where(lane == HD + 1, shift, acc)
        o_ref[...] = jnp.where(lane == HD + 2, norm[0], acc)

    q = q_ref[...]
    attend_block(q, (own, other), limit(q, norm[0]), None, finish)


def attend_early(q, own, other):
    whole = pl.BlockSpec((EARLY, 256), lambda i: (0, 0))
    return pl.pallas_call(
        attend_early_kernel,
        grid=(EARLY // BQ,),
        in_specs=[pl.BlockSpec((BQ, 128), lambda i: (i, 0)), whole, whole],
        out_specs=pl.BlockSpec((BQ, 128), lambda i: (i, 0)),
        out_shape=jax.ShapeDtypeStruct((EARLY, 128), F32),
        scratch_shapes=[pltpu.SMEM((1,), F32)],
        compiler_params=PARAMS,
        cost_estimate=pl.CostEstimate(
            flops=EARLY * EARLY * 256, bytes_accessed=5 * 2**20, transcendentals=0
        ),
        name="attend_early",
    )(q, own, other)


def attend_late_kernel(
    spots, q1, q2, own1, other1, own2, other2, sums, o_ref, norm
):
    block = pl.program_id(0)

    @pl.when(block == 0)
    def _():
        now = jnp.maximum(largest(own2[:, 0:128]), largest(other2[:, 0:128]))
        norm[0] = jnp.maximum(now, jnp.max(sums[0:8, HD + 2 : HD + 3]))

    def finish(shift, acc):
        out = (acc * (1.0 / acc[:, HD : HD + 1])).astype(BF16)
        for t in range(BQ // PART):
            spot = pl.multiple_of(spots[block * (BQ // PART) + t], PART)
            o_ref[pl.ds(spot, PART), :] = out[t * PART : (t + 1) * PART]

    @pl.when(block < EARLY // BQ)
    def _():
        q = q1[...]
        shift = sums[:, HD + 1 : HD + 2]
        settled = jnp.max(jnp.abs(shift)) == 0.0
        attend_block(
            q,
            (own2, other2),
            jnp.logical_and(limit(q, norm[0]), settled),
            lambda: (shift, sums[...]),
            finish,
        )

    @pl.when(block == EARLY // BQ)
    def _():
        q = q2[...]
        attend_block(q, (own1, other1, own2, other2), limit(q, norm[0]), None, finish)


def attend_late(spots, q1, q2, own1, other1, own2, other2, sums):
    last = EARLY // BQ - 1

    def whole(rows, width):
        return pl.BlockSpec((rows, width), lambda i: (0, 0))

    def block(width):
        return pl.BlockSpec((BQ, width), lambda i: (jnp.minimum(i, last), 0))

    total = EARLY + LATE
    return pl.pallas_call(
        attend_late_kernel,
        grid=(total // BQ,),
        in_specs=[
            SMEM,
            block(128),
            whole(LATE, 128),
            whole(EARLY, 256),
            whole(EARLY, 256),
            whole(LATE, 256),
            whole(LATE, 256),
            block(128),
        ],
        out_specs=whole(total, 128),
        out_shape=jax.ShapeDtypeStruct((total, 128), BF16),
        scratch_shapes=[pltpu.SMEM((1,), F32)],
        compiler_params=PARAMS,
        cost_estimate=pl.CostEstimate(
            flops=8 * (total * total - EARLY * EARLY) * 256,
            bytes_accessed=7 * 2**20,
            transcendentals=0,
        ),
        name="attend_late",
    )(spots, q1, q2, own1, other1, own2, other2, sums)


def unpack(target, tiles, k):
    low, high = 12 * k, 12 * k + 12
    for s in range(32):
        parts = []
        for i in range(4):
            for t in range(low // 16, (high - 1) // 16 + 1):
                a, b = max(low - 16 * t, 0), min(high - 16 * t, 16)
                parts.append(tiles[t][4 * s + i, a:b, :])
        target[48 * s : 48 * s + 48, :] = jnp.concatenate(parts, axis=0)


def expand_kernel(
    count, att, frames, gain, weights, after_out, gated_out, rows, t0, t1, t2, w, w2, sems
):
    tiles = (t0, t1, t2)
    copies = [
        pltpu.make_async_copy(weights.at[:, 16 * t : 16 * t + 16, :], tiles[t], sems.at[t])
        for t in range(3)
    ]
    for copy in copies:
        copy.start()
    for h in range(16):
        rows[:, h * HD : (h + 1) * HD] = att[h, :, 0:HD]
    copies[0].wait()
    unpack(w, tiles, 0)
    out_term = jnp.dot(rows[...], w[...], preferred_element_type=F32)
    after = frames[...].astype(F32) + out_term
    after_out[...] = after
    normed = layer_norm(after, gain[...]).astype(BF16)
    copies[1].wait()
    unpack(w2, tiles, 1)
    copies[2].wait()
    unpack(w, tiles, 2)
    real = lax.broadcasted_iota(jnp.int32, (ROWS, 1), 0) < count[0]
    for n in range(3):
        cols = slice(n * 512, (n + 1) * 512)
        left = jnp.dot(normed, w2[:, cols], preferred_element_type=F32)
        right = jnp.dot(normed, w[:, cols], preferred_element_type=F32)
        gate = left * (1.0 / (1.0 + jnp.exp(-right)))
        gated_out[:, cols] = jnp.where(real, gate, 0.0).astype(BF16)


def expand(count, att, frames, gain, weights):
    return pl.pallas_call(
        expand_kernel,
        in_specs=[SMEM, VMEM, VMEM, VMEM, HBM],
        out_specs=(VMEM, VMEM),
        out_shape=(
            jax.ShapeDtypeStruct((ROWS, D), F32),
            jax.ShapeDtypeStruct((ROWS, D), BF16),
        ),
        scratch_shapes=[pltpu.VMEM((ROWS, D), BF16)]
        + [pltpu.VMEM((128, 16, D), BF16)] * 3
        + [pltpu.VMEM((D, D), BF16)] * 2
        + [pltpu.SemaphoreType.DMA((3,))],
        compiler_params=PARAMS,
        cost_estimate=pl.CostEstimate(
            flops=2 * ROWS * D * D * 3, bytes_accessed=20 * 2**20, transcendentals=ROWS * D
        ),
        name="expand",
    )(count, att, frames, gain, weights)


def mix_kernel(gated, taps, weights, mixed, w, wide, tile, sem):
    copy = pltpu.make_async_copy(weights.at[:, 32:48, :], tile, sem)
    copy.start()
    wide[0:16, :] = jnp.zeros((16, D), F32)
    wide[16 : 16 + ROWS, :] = gated[...].astype(F32)
    wide[16 + ROWS : 32 + ROWS, :] = jnp.zeros((16, D), F32)
    for n in range(D // 128):
        cols = slice(n * 128, (n + 1) * 128)
        acc = jnp.zeros((ROWS, 128), F32)
        for s in range(8):
            shifted = wide[s : s + ROWS + 24, cols]
            for a in range(4):
                k = 8 * a + s - 1
                if 0 <= k < KERNEL:
                    acc = acc + shifted[8 * a : 8 * a + ROWS] * taps[k : k + 1, cols]
        mixed[:, cols] = acc
    copy.wait()
    unpack(w, (None, None, tile), 3)


def mix(gated, taps, weights):
    return pl.pallas_call(
        mix_kernel,
        in_specs=[VMEM, VMEM, HBM],
        out_specs=(VMEM, VMEM),
        out_shape=(
            jax.ShapeDtypeStruct((ROWS, D), F32),
            jax.ShapeDtypeStruct((D, D), BF16),
        ),
        scratch_shapes=[
            pltpu.VMEM((ROWS + 32, D), F32),
            pltpu.VMEM((128, 16, D), BF16),
            pltpu.SemaphoreType.DMA,
        ],
        compiler_params=PARAMS,
        cost_estimate=pl.CostEstimate(
            flops=2 * ROWS * D * KERNEL * 16, bytes_accessed=14 * 2**20, transcendentals=0
        ),
        name="mix",
    )(gated, taps, weights)


def down_kernel(mixed, before, behind, after, taps, gain, w, out, wide, head, tail):
    wide[...] = mixed[...]
    head[0:16, :] = before[...].astype(F32)
    head[16:32, :] = jnp.zeros((16, D), F32)
    tail[0:16, :] = jnp.zeros((16, D), F32)
    tail[16:32, :] = behind[...].astype(F32)
    for n in range(D // 128):
        cols = slice(n * 128, (n + 1) * 128)
        top = wide[0:16, cols]
        for k in range(15):
            top = top + head[k + 1 : k + 17, cols] * taps[k : k + 1, cols]
        wide[0:16, cols] = top
        bottom = wide[ROWS - 16 : ROWS, cols]
        for k in range(16, KERNEL):
            bottom = bottom + tail[k - 15 : k + 1, cols] * taps[k : k + 1, cols]
        wide[ROWS - 16 : ROWS, cols] = bottom
    normed = layer_norm(wide[...], gain[...])
    activated = (normed / (1.0 + jnp.exp(-normed))).astype(BF16)
    term = jnp.dot(activated, w[...], preferred_element_type=F32)
    out[...] = (after[...] + term).astype(BF16)


def down(mixed, before, behind, after, taps, gain, w):
    return pl.pallas_call(
        down_kernel,
        in_specs=[VMEM] * 7,
        out_specs=VMEM,
        out_shape=jax.ShapeDtypeStruct((ROWS, D), BF16),
        scratch_shapes=[
            pltpu.VMEM((ROWS, D), F32),
            pltpu.VMEM((32, D), F32),
            pltpu.VMEM((32, D), F32),
        ],
        compiler_params=PARAMS,
        cost_estimate=pl.CostEstimate(
            flops=2 * ROWS * D * D, bytes_accessed=8 * 2**20, transcendentals=ROWS * D
        ),
        name="down",
    )(mixed, before, behind, after, taps, gain, w)


def on_device(
    frames,
    frame_mask,
    attend_gain,
    w_query,
    w_key,
    w_value,
    w_out,
    conv_gain,
    w_expand,
    depth_kernel,
    depth_gain,
    w_down,
):
    x, y, c, z = (lax.axis_index(a) for a in ("x", "y", "c", "z"))
    own_frames = frames[0]

    others = jnp.concatenate([w_out, w_expand[:, :D], w_expand[:, D:], w_down], axis=0)
    weights = lax.all_gather(others, ("x", "y", "c", "z"), axis=0)

    normed = layer_norm(own_frames.astype(F32), attend_gain).astype(BF16)
    lines0 = gathered(normed[:PART], "x")
    lines1 = gathered(normed[PART:], "y")
    early0, late0 = plane(jnp.stack(lines0), "y")
    early1, late1 = plane(jnp.stack(lines1), "x")

    own_count = jnp.sum(frame_mask[0])
    w_query, w_key, w_value, _ = lax.optimization_barrier((w_query, w_key, w_value, lines0[1]))
    heads = jnp.stack([w.reshape(12, 16, HD) for w in (w_query, w_key, w_value)], axis=2)
    heads = jnp.pad(heads, ((0, 4), (0, 0), (0, 0), (0, 128 - HD)))
    heads = heads.reshape(16, 16, 384).transpose(1, 0, 2)
    at_count = (jnp.arange(384) == HD)[None, None, :]
    heads = jnp.where(at_count, own_count.astype(BF16), heads)
    heads = lax.all_to_all(heads, ("x", "y"), split_axis=0, concat_axis=0, tiled=True)
    own_w = jnp.stack(gathered(heads, "z"))
    other_w = pull(own_w, "c", 1)
    chunks, sides = order(x, y)
    counts = jnp.clip(heads[:, 0, HD].astype(jnp.int32)[chunks] - sides * PART, 0, PART)
    place = jnp.stack([c, z]).astype(jnp.int32)

    q1, kv1, w = project_early(place, counts, early0 + early1, own_w, other_w)
    kv1_other = pull(kv1, "c", 1)
    sums = attend_early(q1, kv1, kv1_other)
    w, sums = lax.optimization_barrier((w, sums))
    q2, kv2 = project_late(counts, late0 + late1, w)
    kv2_other = pull(kv2, "c", 1)
    spots = (chunks * ROWS + sides * PART).astype(jnp.int32)
    attended = attend_late(spots, q1, q2, kv1, kv1_other, kv2, kv2_other, sums)
    attended = attended.reshape(16, ROWS, 128)
    attended = lax.all_to_all(attended, ("x", "y"), split_axis=0, concat_axis=0, tiled=True)

    after, gated = expand(
        own_count.reshape(1).astype(jnp.int32), attended, own_frames, conv_gain[None], weights
    )
    line = ("x", "y", "c")
    before = lax.ppermute(gated[ROWS - 16 :], line, [(i, i + 1) for i in range(31)])
    behind = lax.ppermute(gated[:16], line, [(i + 1, i) for i in range(31)])
    mixed, w_last = mix(gated, depth_kernel, weights)
    out = down(mixed, before, behind, after, depth_kernel, depth_gain[None], w_last)
    return out[None]


def solution(mesh):
    cells = Mesh(mesh.devices.reshape(4, 4, 2, 4), ("x", "y", "c", "z"))
    seq = ("x", "y", "c")
    spread = P(("x", "y", "c", "z"), None)
    in_specs = (
        P("z", seq, None),
        P("z", seq),
        P(),
        spread,
        spread,
        spread,
        spread,
        P(),
        spread,
        P(),
        P(),
        spread,
    )
    return jax.shard_map(
        on_device, mesh=cells, in_specs=in_specs, out_specs=P("z", seq, None), check_vma=False
    )
```

```python
import functools
import math

import jax
import jax.numpy as jnp
from jax import lax
from jax.experimental import pallas as pl
from jax.experimental.pallas import tpu as pltpu
from jax.sharding import Mesh, PartitionSpec as P

D = 1536
ROWS = 192
HD = 96
KERNEL = 31
PART = 96
EARLY = 24 * PART
LATE = 8 * PART
BQ = EARLY // 2
BK = 384
SCALE = math.log2(math.e) / math.sqrt(HD)
NEG = -1e30
F32 = jnp.float32
BF16 = jnp.bfloat16
VMEM_LIMIT = 56 * 2**20
VMEM = pl.BlockSpec(memory_space=pltpu.VMEM)
SMEM = pl.BlockSpec(memory_space=pltpu.SMEM)
HBM = pl.BlockSpec(memory_space=pl.ANY)
PARAMS = pltpu.CompilerParams(vmem_limit_bytes=VMEM_LIMIT)


def pull(value, axis, step):
    count = lax.axis_size(axis)
    return lax.ppermute(value, axis, [((i + step) % count, i) for i in range(count)])


def gathered(value, axis):
    return [value] + [pull(value, axis, j) for j in (1, 2, 3)]


def plane(line, outer):
    line = jnp.stack(line)
    after, before = pull(line, outer, 1), pull(line, outer, 3)
    return [line, after, before], [after[:2], before[2:]]


def order(x, y):
    chunks, sides = [], []
    for side in range(2):
        for outer in (0, 1, 3):
            for inner in range(4):
                chunks.append((outer, inner))
                sides.append(side)
    for side in range(2):
        for inner in range(4):
            chunks.append((2, inner))
            sides.append(side)
    outer = jnp.array([o for o, _ in chunks], jnp.int32)
    inner = jnp.array([i for _, i in chunks], jnp.int32)
    side = jnp.array(sides, jnp.int32)
    across = jnp.where(side == 0, inner, outer)
    along = jnp.where(side == 0, outer, inner)
    return (x + across) % 4 * 4 + (y + along) % 4, side


def layer_norm(values, gain):
    center = values - jnp.mean(values, axis=-1, keepdims=True)
    spread = jnp.mean(center * center, axis=-1, keepdims=True)
    return center * lax.rsqrt(spread + 1e-05) * gain


def project_rows(first, counts, rows, w, q_out, kv_out):
    n = rows.shape[0]
    lane = lax.broadcasted_iota(jnp.int32, (PART, 128), 1)
    row = lax.broadcasted_iota(jnp.int32, (PART, 128), 0)
    product = jnp.dot(rows.reshape(n * PART, D), w, preferred_element_type=F32)
    for j in range(n):
        part = product[j * PART : (j + 1) * PART]
        bias = jnp.where(row < counts[first + j], 0.0, NEG)
        span = slice((first + j) % 24 * PART, ((first + j) % 24 + 1) * PART)
        q_out[span, :] = jnp.where(lane == HD, 1.0, part[:, 0:128]).astype(BF16)
        kv_out[span, 0:128] = jnp.where(lane == HD, bias, part[:, 128:256]).astype(BF16)
        kv_out[span, 128:256] = jnp.where(lane == HD, 1.0, part[:, 256:384]).astype(BF16)


def early_kernel(place, counts, *refs):
    pieces, (own_w, other_w, q_out, kv_out, w_out, rows, held, sems) = refs[:6], refs[6:]
    c = place[0]
    w_copies = [
        pltpu.make_async_copy(own_w, held.at[c], sems.at[6]),
        pltpu.make_async_copy(other_w, held.at[1 - c], sems.at[7]),
    ]
    for copy in w_copies:
        copy.start()
    copies = []
    for p in range(6):
        copies.append(
            pltpu.make_async_copy(pieces[p], rows.at[4 * p : 4 * p + 4], sems.at[p])
        )
        copies[-1].start()
    for copy in w_copies:
        copy.wait()
    for chunk in range(16):
        for core in range(2):
            w_out[(chunk * 2 + core) * 48 : (chunk * 2 + core + 1) * 48, :] = jnp.concatenate(
                [held[core, chunk * 4 + k, 0:12, :] for k in range(4)], axis=0
            )
    for side in range(2):
        for p in range(3):
            copies[side * 3 + p].wait()
        project_rows(
            12 * side, counts, rows[12 * side : 12 * side + 12], w_out[...], q_out, kv_out
        )


def project_early(place, counts, pieces, own_w, other_w):
    return pl.pallas_call(
        early_kernel,
        in_specs=[SMEM, SMEM] + [HBM] * 8,
        out_specs=(VMEM, VMEM, VMEM),
        out_shape=(
            jax.ShapeDtypeStruct((EARLY, 128), BF16),
            jax.ShapeDtypeStruct((EARLY, 256), BF16),
            jax.ShapeDtypeStruct((D, 384), BF16),
        ),
        scratch_shapes=[
            pltpu.VMEM((24, PART, D), BF16),
            pltpu.VMEM((2, 64, 16, 384), BF16),
            pltpu.SemaphoreType.DMA((8,)),
        ],
        compiler_params=PARAMS,
        cost_estimate=pl.CostEstimate(
            flops=EARLY * D * 128, bytes_accessed=2**20, transcendentals=0
        ),
        name="project_early",
    )(place, counts, *pieces, own_w, other_w)


def late_kernel(counts, p0, p1, p2, p3, w, q_out, kv_out, rows, sems):
    copies = [
        pltpu.make_async_copy(p, rows.at[2 * i : 2 * i + 2], sems.at[i])
        for i, p in enumerate((p0, p1, p2, p3))
    ]
    for copy in copies:
        copy.start()
    for copy in copies:
        copy.wait()
    project_rows(24, counts, rows[...], w[...], q_out, kv_out)


def project_late(counts, pieces, w):
    return pl.pallas_call(
        late_kernel,
        in_specs=[SMEM] + [HBM] * 4 + [VMEM],
        out_specs=(VMEM, VMEM),
        out_shape=(
            jax.ShapeDtypeStruct((LATE, 128), BF16),
            jax.ShapeDtypeStruct((LATE, 256), BF16),
        ),
        scratch_shapes=[pltpu.VMEM((8, PART, D), BF16), pltpu.SemaphoreType.DMA((4,))],
        compiler_params=PARAMS,
        cost_estimate=pl.CostEstimate(
            flops=2 * LATE * D * 512, bytes_accessed=4 * 2**20, transcendentals=0
        ),
        name="project_late",
    )(counts, *pieces, w)


def largest(rows):
    wide = rows.astype(F32)
    lane = lax.broadcasted_iota(jnp.int32, wide.shape, 1)
    square = jnp.where(lane < HD, wide * wide, 0.0).astype(BF16)
    sums = jnp.dot(square, jnp.ones((128, 128), BF16), preferred_element_type=F32)
    return jnp.max(jnp.max(sums.reshape(-1, 8, 128), axis=0)) * 1.02


def attend_block(q, sources, bounded, first, finish):
    rows = q.shape[0]
    def scores(ref, start):
        return lax.dot_general(
            q,
            ref[pl.ds(start, BK), 0:128],
            (((1,), (1,)), ((), ())),
            preferred_element_type=F32,
        )

    def start_values():
        if first is None:
            return jnp.full((rows, 1), -3e38, F32), jnp.zeros((rows, 128), F32)
        return first()

    @pl.when(bounded)
    def _():
        acc = start_values()[1]
        for ref in sources:
            for i in range(ref.shape[0] // BK):
                p = jnp.exp2(scores(ref, i * BK) * SCALE).astype(BF16)
                acc = acc + jnp.dot(
                    p, ref[pl.ds(i * BK, BK), 128:256], preferred_element_type=F32
                )
        finish(jnp.zeros((rows, 1), F32), acc)

    @pl.when(jnp.logical_not(bounded))
    def _():
        def body(ref, i, carry):
            peak, acc = carry
            start = pl.multiple_of(i * BK, BK)
            s = scores(ref, start) * SCALE
            higher = jnp.maximum(peak, jnp.max(s, axis=1, keepdims=True))
            p = jnp.exp2(s - higher).astype(BF16)
            acc = acc * jnp.exp2(peak - higher) + jnp.dot(
                p, ref[pl.ds(start, BK), 128:256], preferred_element_type=F32
            )
            return higher, acc

        carry = start_values()
        for ref in sources:
            carry = lax.fori_loop(
                0, ref.shape[0] // BK, functools.partial(body, ref), carry
            )
        finish(*carry)


def limit(q, norm):
    return largest(q) * norm <= 60.0 * 60.0 * HD


def attend_early_kernel(q_ref, own, other, o_ref, norm):
    @pl.when(pl.program_id(0) == 0)
    def _():
        norm[0] = jnp.maximum(largest(own[:, 0:128]), largest(other[:, 0:128]))

    def finish(shift, acc):
        lane = lax.broadcasted_iota(jnp.int32, (BQ, 128), 1)
        acc = jnp.where(lane == HD + 1, shift, acc)
        o_ref[...] = jnp.where(lane == HD + 2, norm[0], acc)

    q = q_ref[...]
    attend_block(q, (own, other), limit(q, norm[0]), None, finish)


def attend_early(q, own, other):
    whole = pl.BlockSpec((EARLY, 256), lambda i: (0, 0))
    return pl.pallas_call(
        attend_early_kernel,
        grid=(EARLY // BQ,),
        in_specs=[pl.BlockSpec((BQ, 128), lambda i: (i, 0)), whole, whole],
        out_specs=pl.BlockSpec((BQ, 128), lambda i: (i, 0)),
        out_shape=jax.ShapeDtypeStruct((EARLY, 128), F32),
        scratch_shapes=[pltpu.SMEM((1,), F32)],
        compiler_params=PARAMS,
        cost_estimate=pl.CostEstimate(
            flops=EARLY * EARLY * 256, bytes_accessed=5 * 2**20, transcendentals=0
        ),
        name="attend_early",
    )(q, own, other)


def attend_late_kernel(
    spots, q1, q2, own1, other1, own2, other2, sums, o_ref, norm
):
    block = pl.program_id(0)

    @pl.when(block == 0)
    def _():
        now = jnp.maximum(largest(own2[:, 0:128]), largest(other2[:, 0:128]))
        norm[0] = jnp.maximum(now, jnp.max(sums[0:8, HD + 2 : HD + 3]))

    def finish(shift, acc):
        out = (acc * (1.0 / acc[:, HD : HD + 1])).astype(BF16)
        for t in range(acc.shape[0] // PART):
            spot = pl.multiple_of(spots[block * (BQ // PART) + t], PART)
            o_ref[pl.ds(spot, PART), :] = out[t * PART : (t + 1) * PART]

    @pl.when(block < EARLY // BQ)
    def _():
        q = q1[...]
        shift = sums[:, HD + 1 : HD + 2]
        settled = jnp.max(jnp.abs(shift)) == 0.0
        attend_block(
            q,
            (own2, other2),
            jnp.logical_and(limit(q, norm[0]), settled),
            lambda: (shift, sums[...]),
            finish,
        )

    @pl.when(block == EARLY // BQ)
    def _():
        q = q2[...]
        attend_block(q, (own1, other1, own2, other2), limit(q, norm[0]), None, finish)


def attend_late(spots, q1, q2, own1, other1, own2, other2, sums):
    last = EARLY // BQ - 1

    def whole(rows, width):
        return pl.BlockSpec((rows, width), lambda i: (0, 0))

    def block(width):
        return pl.BlockSpec((BQ, width), lambda i: (jnp.minimum(i, last), 0))

    total = EARLY + LATE
    return pl.pallas_call(
        attend_late_kernel,
        grid=(EARLY // BQ + 1,),
        in_specs=[
            SMEM,
            block(128),
            whole(LATE, 128),
            whole(EARLY, 256),
            whole(EARLY, 256),
            whole(LATE, 256),
            whole(LATE, 256),
            block(128),
        ],
        out_specs=whole(total, 128),
        out_shape=jax.ShapeDtypeStruct((total, 128), BF16),
        scratch_shapes=[pltpu.SMEM((1,), F32)],
        compiler_params=PARAMS,
        cost_estimate=pl.CostEstimate(
            flops=8 * (total * total - EARLY * EARLY) * 256,
            bytes_accessed=7 * 2**20,
            transcendentals=0,
        ),
        name="attend_late",
    )(spots, q1, q2, own1, other1, own2, other2, sums)


def unpack(target, tiles, k):
    low, high = 12 * k, 12 * k + 12
    for s in range(32):
        parts = []
        for i in range(4):
            for t in range(low // 16, (high - 1) // 16 + 1):
                a, b = max(low - 16 * t, 0), min(high - 16 * t, 16)
                parts.append(tiles[t][4 * s + i, a:b, :])
        target[48 * s : 48 * s + 48, :] = jnp.concatenate(parts, axis=0)


def expand_kernel(
    count, att, frames, gain, weights, after_out, gated_out, rows, t0, t1, t2, w, w2, sems
):
    tiles = (t0, t1, t2)
    copies = [
        pltpu.make_async_copy(weights.at[:, 16 * t : 16 * t + 16, :], tiles[t], sems.at[t])
        for t in range(3)
    ]
    for copy in copies:
        copy.start()
    for h in range(16):
        rows[:, h * HD : (h + 1) * HD] = att[h, :, 0:HD]
    copies[0].wait()
    unpack(w, tiles, 0)
    out_term = jnp.dot(rows[...], w[...], preferred_element_type=F32)
    after = frames[...].astype(F32) + out_term
    after_out[...] = after
    normed = layer_norm(after, gain[...]).astype(BF16)
    copies[1].wait()
    unpack(w2, tiles, 1)
    copies[2].wait()
    unpack(w, tiles, 2)
    real = lax.broadcasted_iota(jnp.int32, (ROWS, 1), 0) < count[0]
    for n in range(3):
        cols = slice(n * 512, (n + 1) * 512)
        left = jnp.dot(normed, w2[:, cols], preferred_element_type=F32)
        right = jnp.dot(normed, w[:, cols], preferred_element_type=F32)
        gate = left * (1.0 / (1.0 + jnp.exp(-right)))
        gated_out[:, cols] = jnp.where(real, gate, 0.0).astype(BF16)


def expand(count, att, frames, gain, weights):
    return pl.pallas_call(
        expand_kernel,
        in_specs=[SMEM, VMEM, VMEM, VMEM, HBM],
        out_specs=(VMEM, VMEM),
        out_shape=(
            jax.ShapeDtypeStruct((ROWS, D), F32),
            jax.ShapeDtypeStruct((ROWS, D), BF16),
        ),
        scratch_shapes=[pltpu.VMEM((ROWS, D), BF16)]
        + [pltpu.VMEM((128, 16, D), BF16)] * 3
        + [pltpu.VMEM((D, D), BF16)] * 2
        + [pltpu.SemaphoreType.DMA((3,))],
        compiler_params=PARAMS,
        cost_estimate=pl.CostEstimate(
            flops=2 * ROWS * D * D * 3, bytes_accessed=20 * 2**20, transcendentals=ROWS * D
        ),
        name="expand",
    )(count, att, frames, gain, weights)


def mix_kernel(gated, taps, weights, mixed, w, wide, tile, sem):
    copy = pltpu.make_async_copy(weights.at[:, 32:48, :], tile, sem)
    copy.start()
    wide[0:16, :] = jnp.zeros((16, D), F32)
    wide[16 : 16 + ROWS, :] = gated[...].astype(F32)
    wide[16 + ROWS : 32 + ROWS, :] = jnp.zeros((16, D), F32)
    for n in range(D // 128):
        cols = slice(n * 128, (n + 1) * 128)
        acc = jnp.zeros((ROWS, 128), F32)
        for s in range(8):
            shifted = wide[s : s + ROWS + 24, cols]
            for a in range(4):
                k = 8 * a + s - 1
                if 0 <= k < KERNEL:
                    acc = acc + shifted[8 * a : 8 * a + ROWS] * taps[k : k + 1, cols]
        mixed[:, cols] = acc
    copy.wait()
    unpack(w, (None, None, tile), 3)


def mix(gated, taps, weights):
    return pl.pallas_call(
        mix_kernel,
        in_specs=[VMEM, VMEM, HBM],
        out_specs=(VMEM, VMEM),
        out_shape=(
            jax.ShapeDtypeStruct((ROWS, D), F32),
            jax.ShapeDtypeStruct((D, D), BF16),
        ),
        scratch_shapes=[
            pltpu.VMEM((ROWS + 32, D), F32),
            pltpu.VMEM((128, 16, D), BF16),
            pltpu.SemaphoreType.DMA,
        ],
        compiler_params=PARAMS,
        cost_estimate=pl.CostEstimate(
            flops=2 * ROWS * D * KERNEL * 16, bytes_accessed=14 * 2**20, transcendentals=0
        ),
        name="mix",
    )(gated, taps, weights)


def down_kernel(mixed, before, behind, after, taps, gain, w, out, wide, head, tail):
    wide[...] = mixed[...]
    head[0:16, :] = before[...].astype(F32)
    head[16:32, :] = jnp.zeros((16, D), F32)
    tail[0:16, :] = jnp.zeros((16, D), F32)
    tail[16:32, :] = behind[...].astype(F32)
    for n in range(D // 128):
        cols = slice(n * 128, (n + 1) * 128)
        top = wide[0:16, cols]
        for k in range(15):
            top = top + head[k + 1 : k + 17, cols] * taps[k : k + 1, cols]
        wide[0:16, cols] = top
        bottom = wide[ROWS - 16 : ROWS, cols]
        for k in range(16, KERNEL):
            bottom = bottom + tail[k - 15 : k + 1, cols] * taps[k : k + 1, cols]
        wide[ROWS - 16 : ROWS, cols] = bottom
    normed = layer_norm(wide[...], gain[...])
    activated = (normed / (1.0 + jnp.exp(-normed))).astype(BF16)
    term = jnp.dot(activated, w[...], preferred_element_type=F32)
    out[...] = (after[...] + term).astype(BF16)


def down(mixed, before, behind, after, taps, gain, w):
    return pl.pallas_call(
        down_kernel,
        in_specs=[VMEM] * 7,
        out_specs=VMEM,
        out_shape=jax.ShapeDtypeStruct((ROWS, D), BF16),
        scratch_shapes=[
            pltpu.VMEM((ROWS, D), F32),
            pltpu.VMEM((32, D), F32),
            pltpu.VMEM((32, D), F32),
        ],
        compiler_params=PARAMS,
        cost_estimate=pl.CostEstimate(
            flops=2 * ROWS * D * D, bytes_accessed=8 * 2**20, transcendentals=ROWS * D
        ),
        name="down",
    )(mixed, before, behind, after, taps, gain, w)


def on_device(
    frames,
    frame_mask,
    attend_gain,
    w_query,
    w_key,
    w_value,
    w_out,
    conv_gain,
    w_expand,
    depth_kernel,
    depth_gain,
    w_down,
):
    x, y, c, z = (lax.axis_index(a) for a in ("x", "y", "c", "z"))
    own_frames = frames[0]

    others = jnp.concatenate([w_out, w_expand[:, :D], w_expand[:, D:], w_down], axis=0)
    weights = lax.all_gather(others, ("x", "y", "c", "z"), axis=0)

    normed = layer_norm(own_frames.astype(F32), attend_gain).astype(BF16)
    early0, pass0 = plane(gathered(normed[:PART], "x"), "y")
    early1, pass1 = plane(gathered(normed[PART:], "y"), "x")
    early, passed = lax.optimization_barrier((early0 + early1, pass0 + pass1))
    late = [pull(p, a, j) for p, a, j in zip(passed, ("y", "y", "x", "x"), (1, 3, 1, 3))]

    own_count = jnp.sum(frame_mask[0])
    heads = jnp.stack([w.reshape(12, 16, HD) for w in (w_query, w_key, w_value)], axis=2)
    heads = jnp.pad(heads, ((0, 4), (0, 0), (0, 0), (0, 128 - HD)))
    heads = heads.reshape(16, 16, 384).transpose(1, 0, 2)
    at_count = (jnp.arange(384) == HD)[None, None, :]
    heads = jnp.where(at_count, own_count.astype(BF16), heads)
    heads = jnp.broadcast_to(heads[:, None], (16, 4, 16, 384)).reshape(64, 16, 384)
    own_w = lax.all_to_all(heads, ("x", "y", "z"), split_axis=0, concat_axis=0, tiled=True)
    other_w = pull(own_w, "c", 1)
    counts = lax.dynamic_index_in_dim(
        own_w[:, 0, HD].reshape(16, 4), z, 1, keepdims=False
    ).astype(jnp.int32)
    chunks, sides = order(x, y)
    counts = jnp.clip(counts[chunks] - sides * PART, 0, PART)
    place = c.reshape(1).astype(jnp.int32)

    q1, kv1, w = project_early(place, counts, early, own_w, other_w)
    kv1_other = pull(kv1, "c", 1)
    sums = attend_early(q1, kv1, kv1_other)
    w, sums = lax.optimization_barrier((w, sums))
    q2, kv2 = project_late(counts, late, w)
    kv2_other = pull(kv2, "c", 1)
    spots = (chunks * ROWS + sides * PART).astype(jnp.int32)
    attended = attend_late(spots, q1, q2, kv1, kv1_other, kv2, kv2_other, sums)
    attended = attended.reshape(16, ROWS, 128)
    attended = lax.all_to_all(attended, ("x", "y"), split_axis=0, concat_axis=0, tiled=True)

    after, gated = expand(
        own_count.reshape(1).astype(jnp.int32), attended, own_frames, conv_gain[None], weights
    )
    line = ("x", "y", "c")
    before = lax.ppermute(gated[ROWS - 16 :], line, [(i, i + 1) for i in range(31)])
    behind = lax.ppermute(gated[:16], line, [(i + 1, i) for i in range(31)])
    mixed, w_last = mix(gated, depth_kernel, weights)
    out = down(mixed, before, behind, after, depth_kernel, depth_gain[None], w_last)
    return out[None]


def solution(mesh):
    cells = Mesh(mesh.devices.reshape(4, 4, 2, 4), ("x", "y", "c", "z"))
    seq = ("x", "y", "c")
    spread = P(("x", "y", "c", "z"), None)
    in_specs = (
        P("z", seq, None),
        P("z", seq),
        P(),
        spread,
        spread,
        spread,
        spread,
        P(),
        spread,
        P(),
        P(),
        spread,
    )
    return jax.shard_map(
        on_device, mesh=cells, in_specs=in_specs, out_specs=P("z", seq, None), check_vma=False
    )
```

```python
import functools
import math

import jax
import jax.numpy as jnp
from jax import lax
from jax.experimental import pallas as pl
from jax.experimental.pallas import tpu as pltpu
from jax.sharding import Mesh, PartitionSpec as P

D = 1536
ROWS = 192
HD = 96
KERNEL = 31
PART = 96
EARLY = 24 * PART
LATE = 8 * PART
BQ = EARLY // 2
BK = 384
SCALE = math.log2(math.e) / math.sqrt(HD)
NEG = -1e30
F32 = jnp.float32
BF16 = jnp.bfloat16
VMEM_LIMIT = 56 * 2**20
VMEM = pl.BlockSpec(memory_space=pltpu.VMEM)
SMEM = pl.BlockSpec(memory_space=pltpu.SMEM)
HBM = pl.BlockSpec(memory_space=pl.ANY)
PARAMS = pltpu.CompilerParams(vmem_limit_bytes=VMEM_LIMIT)


def pull(value, axis, step):
    count = lax.axis_size(axis)
    return lax.ppermute(value, axis, [((i + step) % count, i) for i in range(count)])


def gathered(value, axis):
    return [value] + [pull(value, axis, j) for j in (1, 2, 3)]


def plane(line, outer):
    line = jnp.stack(line)
    return [line, pull(line, outer, 1), pull(line, outer, 3)]


def parts():
    early = [
        (0, i, o) if side == 0 else (1, o, i)
        for side in range(2)
        for o in (0, 1, 3)
        for i in range(4)
    ]
    return early + [(0, i, 2) for i in range(4)] + [(1, 2, i) for i in range(4)]


def where_part(part):
    side, across, along = parts()[part]
    x, y = lax.axis_index("x"), lax.axis_index("y")
    return (x + across) % 4 * 4 + (y + along) % 4, side


def layer_norm(values, gain):
    center = values - jnp.mean(values, axis=-1, keepdims=True)
    spread = jnp.mean(center * center, axis=-1, keepdims=True)
    return center * lax.rsqrt(spread + 1e-05) * gain


def prepare_kernel(
    frames, mask, gain, wq, wk, wv, wo, we, wd, top, bottom, heads, others
):
    normed = layer_norm(frames[...].astype(F32), gain[...]).astype(BF16)
    top[...] = normed[:PART]
    bottom[...] = normed[PART:]
    count = jnp.sum(mask[...].astype(F32))
    lane = lax.broadcasted_iota(jnp.int32, (12, 128), 1)
    fill = jnp.where(lane == HD, count, 0.0).astype(BF16)
    heads[...] = jnp.zeros(heads.shape, BF16)
    for m, w in enumerate((wq, wk, wv)):
        for h in range(16):
            part = jnp.concatenate([w[:, h * HD : (h + 1) * HD], fill[:, HD:]], axis=1)
            heads[h, 0:12, m * 128 : (m + 1) * 128] = part
    others[...] = jnp.concatenate([wo[...], we[:, 0:D], we[:, D : 2 * D], wd[...]], axis=0)


def prepare(frames, mask, gain, wq, wk, wv, wo, we, wd):
    return pl.pallas_call(
        prepare_kernel,
        in_specs=[VMEM] * 9,
        out_specs=(VMEM,) * 4,
        out_shape=(
            jax.ShapeDtypeStruct((PART, D), BF16),
            jax.ShapeDtypeStruct((PART, D), BF16),
            jax.ShapeDtypeStruct((16, 16, 384), BF16),
            jax.ShapeDtypeStruct((48, D), BF16),
        ),
        compiler_params=PARAMS,
        name="prepare",
    )(frames, mask, gain, wq, wk, wv, wo, we, wd)


def project_rows(first, counts, rows, w, q_out, kv_out):
    n = rows.shape[0]
    lane = lax.broadcasted_iota(jnp.int32, (PART, 128), 1)
    row = lax.broadcasted_iota(jnp.int32, (PART, 128), 0)
    product = jnp.dot(rows.reshape(n * PART, D), w, preferred_element_type=F32)
    for j in range(n):
        part = product[j * PART : (j + 1) * PART]
        chunk, side = where_part(first + j)
        bias = jnp.where(row < counts[chunk] - side * PART, 0.0, NEG)
        span = slice((first + j) % 24 * PART, ((first + j) % 24 + 1) * PART)
        q_out[span, :] = jnp.where(lane == HD, 1.0, part[:, 0:128]).astype(BF16)
        kv_out[span, 0:128] = jnp.where(lane == HD, bias, part[:, 128:256]).astype(BF16)
        kv_out[span, 128:256] = jnp.where(lane == HD, 1.0, part[:, 256:384]).astype(BF16)


def early_kernel(counts, *refs):
    pieces, (own_w, other_w, q_out, kv_out, w_out), passed = refs[:6], refs[6:11], refs[11:15]
    rows, held, sems = refs[15:]
    c, z = lax.axis_index("c"), lax.axis_index("z")
    w_copies = [
        pltpu.make_async_copy(own_w, held.at[c], sems.at[6]),
        pltpu.make_async_copy(other_w, held.at[1 - c], sems.at[7]),
    ]
    for copy in w_copies:
        copy.start()
    copies = []
    for p in range(6):
        copies.append(
            pltpu.make_async_copy(pieces[p], rows.at[4 * p : 4 * p + 4], sems.at[p])
        )
        copies[-1].start()
    for copy in w_copies:
        copy.wait()
    for chunk in range(16):
        for core in range(2):
            w_out[(chunk * 2 + core) * 48 : (chunk * 2 + core + 1) * 48, :] = jnp.concatenate(
                [
                    held[core, (k - z) % 4, chunk, 0:12, :]
                    for k in range(4)
                ],
                axis=0,
            )
    onward = []
    for side in range(2):
        for p in range(3):
            copies[side * 3 + p].wait()
        for k, first in ((0, 4), (1, 10)):
            first = first + 12 * side
            onward.append(
                pltpu.make_async_copy(
                    rows.at[first : first + 2], passed[2 * side + k], sems.at[8 + 2 * side + k]
                )
            )
            onward[-1].start()
        project_rows(
            12 * side, counts, rows[12 * side : 12 * side + 12], w_out[...], q_out, kv_out
        )
    for copy in onward:
        copy.wait()


def project_early(counts, pieces, own_w, other_w):
    return pl.pallas_call(
        early_kernel,
        in_specs=[SMEM] + [HBM] * 8,
        out_specs=(VMEM, VMEM, VMEM, HBM, HBM, HBM, HBM),
        out_shape=(
            jax.ShapeDtypeStruct((EARLY, 128), BF16),
            jax.ShapeDtypeStruct((EARLY, 256), BF16),
            jax.ShapeDtypeStruct((D, 384), BF16),
        )
        + (jax.ShapeDtypeStruct((2, PART, D), BF16),) * 4,
        scratch_shapes=[
            pltpu.VMEM((24, PART, D), BF16),
            pltpu.VMEM((2, 4, 16, 16, 384), BF16),
            pltpu.SemaphoreType.DMA((12,)),
        ],
        compiler_params=PARAMS,
        cost_estimate=pl.CostEstimate(
            flops=EARLY * D * 128, bytes_accessed=2**20, transcendentals=0
        ),
        name="project_early",
    )(counts, *pieces, own_w, other_w)


def late_kernel(counts, p0, p1, p2, p3, w, q_out, kv_out, rows, sems):
    copies = [
        pltpu.make_async_copy(p, rows.at[2 * i : 2 * i + 2], sems.at[i])
        for i, p in enumerate((p0, p1, p2, p3))
    ]
    for copy in copies:
        copy.start()
    for copy in copies:
        copy.wait()
    project_rows(24, counts, rows[...], w[...], q_out, kv_out)


def project_late(counts, pieces, w):
    return pl.pallas_call(
        late_kernel,
        in_specs=[SMEM] + [HBM] * 4 + [VMEM],
        out_specs=(VMEM, VMEM),
        out_shape=(
            jax.ShapeDtypeStruct((LATE, 128), BF16),
            jax.ShapeDtypeStruct((LATE, 256), BF16),
        ),
        scratch_shapes=[pltpu.VMEM((8, PART, D), BF16), pltpu.SemaphoreType.DMA((4,))],
        compiler_params=PARAMS,
        cost_estimate=pl.CostEstimate(
            flops=2 * LATE * D * 512, bytes_accessed=4 * 2**20, transcendentals=0
        ),
        name="project_late",
    )(counts, *pieces, w)


def largest(rows):
    wide = rows.astype(F32)
    lane = lax.broadcasted_iota(jnp.int32, wide.shape, 1)
    square = jnp.where(lane < HD, wide * wide, 0.0).astype(BF16)
    sums = jnp.dot(square, jnp.ones((128, 128), BF16), preferred_element_type=F32)
    return jnp.max(jnp.max(sums.reshape(-1, 8, 128), axis=0)) * 1.02


def attend_block(q, sources, bounded, first, finish):
    rows = q.shape[0]
    def scores(ref, start):
        return lax.dot_general(
            q,
            ref[pl.ds(start, BK), 0:128],
            (((1,), (1,)), ((), ())),
            preferred_element_type=F32,
        )

    def start_values():
        if first is None:
            return jnp.full((rows, 1), -3e38, F32), jnp.zeros((rows, 128), F32)
        return first()

    @pl.when(bounded)
    def _():
        acc = start_values()[1]
        for ref in sources:
            for i in range(ref.shape[0] // BK):
                p = jnp.exp2(scores(ref, i * BK) * SCALE).astype(BF16)
                acc = acc + jnp.dot(
                    p, ref[pl.ds(i * BK, BK), 128:256], preferred_element_type=F32
                )
        finish(jnp.zeros((rows, 1), F32), acc)

    @pl.when(jnp.logical_not(bounded))
    def _():
        def body(ref, i, carry):
            peak, acc = carry
            start = pl.multiple_of(i * BK, BK)
            s = scores(ref, start) * SCALE
            higher = jnp.maximum(peak, jnp.max(s, axis=1, keepdims=True))
            p = jnp.exp2(s - higher).astype(BF16)
            acc = acc * jnp.exp2(peak - higher) + jnp.dot(
                p, ref[pl.ds(start, BK), 128:256], preferred_element_type=F32
            )
            return higher, acc

        carry = start_values()
        for ref in sources:
            carry = lax.fori_loop(
                0, ref.shape[0] // BK, functools.partial(body, ref), carry
            )
        finish(*carry)


def limit(q, norm):
    return largest(q) * norm <= 60.0 * 60.0 * HD


def attend_early_kernel(q_ref, own, other, o_ref, norm):
    @pl.when(pl.program_id(0) == 0)
    def _():
        norm[0] = jnp.maximum(largest(own[:, 0:128]), largest(other[:, 0:128]))

    def finish(shift, acc):
        lane = lax.broadcasted_iota(jnp.int32, (BQ, 128), 1)
        acc = jnp.where(lane == HD + 1, shift, acc)
        o_ref[...] = jnp.where(lane == HD + 2, norm[0], acc)

    q = q_ref[...]
    attend_block(q, (own, other), limit(q, norm[0]), None, finish)


def attend_early(q, own, other):
    whole = pl.BlockSpec((EARLY, 256), lambda i: (0, 0))
    return pl.pallas_call(
        attend_early_kernel,
        grid=(EARLY // BQ,),
        in_specs=[pl.BlockSpec((BQ, 128), lambda i: (i, 0)), whole, whole],
        out_specs=pl.BlockSpec((BQ, 128), lambda i: (i, 0)),
        out_shape=jax.ShapeDtypeStruct((EARLY, 128), F32),
        scratch_shapes=[pltpu.SMEM((1,), F32)],
        compiler_params=PARAMS,
        cost_estimate=pl.CostEstimate(
            flops=EARLY * EARLY * 256, bytes_accessed=5 * 2**20, transcendentals=0
        ),
        name="attend_early",
    )(q, own, other)


def attend_late_kernel(q1, q2, own1, other1, own2, other2, sums, o_ref, norm):
    block = pl.program_id(0)

    @pl.when(block == 0)
    def _():
        now = jnp.maximum(largest(own2[:, 0:128]), largest(other2[:, 0:128]))
        norm[0] = jnp.maximum(now, jnp.max(sums[0:8, HD + 2 : HD + 3]))

    def finish(number, shift, acc):
        out = (acc * (1.0 / acc[:, HD : HD + 1])).astype(BF16)
        for t in range(acc.shape[0] // PART):
            chunk, side = where_part(number * (BQ // PART) + t)
            spot = pl.multiple_of(chunk * ROWS + side * PART, PART)
            o_ref[pl.ds(spot, PART), :] = out[t * PART : (t + 1) * PART]

    for number in range(EARLY // BQ):

        @pl.when(block == number)
        def _(number=number):
            q = q1[...]
            shift = sums[:, HD + 1 : HD + 2]
            settled = jnp.max(jnp.abs(shift)) == 0.0
            attend_block(
                q,
                (own2, other2),
                jnp.logical_and(limit(q, norm[0]), settled),
                lambda: (shift, sums[...]),
                functools.partial(finish, number),
            )

    @pl.when(block == EARLY // BQ)
    def _():
        q = q2[...]
        attend_block(
            q,
            (own1, other1, own2, other2),
            limit(q, norm[0]),
            None,
            functools.partial(finish, EARLY // BQ),
        )


def attend_late(q1, q2, own1, other1, own2, other2, sums):
    last = EARLY // BQ - 1

    def whole(rows, width):
        return pl.BlockSpec((rows, width), lambda i: (0, 0))

    def block(width):
        return pl.BlockSpec((BQ, width), lambda i: (jnp.minimum(i, last), 0))

    total = EARLY + LATE
    return pl.pallas_call(
        attend_late_kernel,
        grid=(EARLY // BQ + 1,),
        in_specs=[
            block(128),
            whole(LATE, 128),
            whole(EARLY, 256),
            whole(EARLY, 256),
            whole(LATE, 256),
            whole(LATE, 256),
            block(128),
        ],
        out_specs=whole(total, 128),
        out_shape=jax.ShapeDtypeStruct((total, 128), BF16),
        scratch_shapes=[pltpu.SMEM((1,), F32)],
        compiler_params=PARAMS,
        cost_estimate=pl.CostEstimate(
            flops=8 * (total * total - EARLY * EARLY) * 256,
            bytes_accessed=7 * 2**20,
            transcendentals=0,
        ),
        name="attend_late",
    )(q1, q2, own1, other1, own2, other2, sums)


def unpack(target, tiles, k):
    low, high = 12 * k, 12 * k + 12
    for s in range(32):
        parts = []
        for i in range(4):
            for t in range(low // 16, (high - 1) // 16 + 1):
                a, b = max(low - 16 * t, 0), min(high - 16 * t, 16)
                parts.append(tiles[t][4 * s + i, a:b, :])
        target[48 * s : 48 * s + 48, :] = jnp.concatenate(parts, axis=0)


def expand_kernel(
    mask, att, frames, gain, weights, after_out, gated_out, rows, t0, t1, t2, w, w2, sems
):
    tiles = (t0, t1, t2)
    copies = [
        pltpu.make_async_copy(weights.at[:, 16 * t : 16 * t + 16, :], tiles[t], sems.at[t])
        for t in range(3)
    ]
    for copy in copies:
        copy.start()
    for h in range(16):
        rows[:, h * HD : (h + 1) * HD] = att[h, :, 0:HD]
    copies[0].wait()
    unpack(w, tiles, 0)
    out_term = jnp.dot(rows[...], w[...], preferred_element_type=F32)
    after = frames[...].astype(F32) + out_term
    after_out[...] = after
    normed = layer_norm(after, gain[...]).astype(BF16)
    copies[1].wait()
    unpack(w2, tiles, 1)
    copies[2].wait()
    unpack(w, tiles, 2)
    count = jnp.sum(mask[...].astype(F32))
    real = lax.broadcasted_iota(jnp.int32, (ROWS, 1), 0).astype(F32) < count
    for n in range(3):
        cols = slice(n * 512, (n + 1) * 512)
        left = jnp.dot(normed, w2[:, cols], preferred_element_type=F32)
        right = jnp.dot(normed, w[:, cols], preferred_element_type=F32)
        gate = left * (1.0 / (1.0 + jnp.exp(-right)))
        gated_out[:, cols] = jnp.where(real, gate, 0.0).astype(BF16)


def expand(mask, att, frames, gain, weights):
    return pl.pallas_call(
        expand_kernel,
        in_specs=[VMEM, VMEM, VMEM, VMEM, HBM],
        out_specs=(VMEM, VMEM),
        out_shape=(
            jax.ShapeDtypeStruct((ROWS, D), F32),
            jax.ShapeDtypeStruct((ROWS, D), BF16),
        ),
        scratch_shapes=[pltpu.VMEM((ROWS, D), BF16)]
        + [pltpu.VMEM((128, 16, D), BF16)] * 3
        + [pltpu.VMEM((D, D), BF16)] * 2
        + [pltpu.SemaphoreType.DMA((3,))],
        compiler_params=PARAMS,
        cost_estimate=pl.CostEstimate(
            flops=2 * ROWS * D * D * 3, bytes_accessed=20 * 2**20, transcendentals=ROWS * D
        ),
        name="expand",
    )(mask, att, frames, gain, weights)


def mix_kernel(gated, taps, weights, mixed, w, wide, tile, sem):
    copy = pltpu.make_async_copy(weights.at[:, 32:48, :], tile, sem)
    copy.start()
    wide[0:16, :] = jnp.zeros((16, D), F32)
    wide[16 : 16 + ROWS, :] = gated[...].astype(F32)
    wide[16 + ROWS : 32 + ROWS, :] = jnp.zeros((16, D), F32)
    for n in range(D // 128):
        cols = slice(n * 128, (n + 1) * 128)
        acc = jnp.zeros((ROWS, 128), F32)
        for s in range(8):
            shifted = wide[s : s + ROWS + 24, cols]
            for a in range(4):
                k = 8 * a + s - 1
                if 0 <= k < KERNEL:
                    acc = acc + shifted[8 * a : 8 * a + ROWS] * taps[k : k + 1, cols]
        mixed[:, cols] = acc
    copy.wait()
    unpack(w, (None, None, tile), 3)


def mix(gated, taps, weights):
    return pl.pallas_call(
        mix_kernel,
        in_specs=[VMEM, VMEM, HBM],
        out_specs=(VMEM, VMEM),
        out_shape=(
            jax.ShapeDtypeStruct((ROWS, D), F32),
            jax.ShapeDtypeStruct((D, D), BF16),
        ),
        scratch_shapes=[
            pltpu.VMEM((ROWS + 32, D), F32),
            pltpu.VMEM((128, 16, D), BF16),
            pltpu.SemaphoreType.DMA,
        ],
        compiler_params=PARAMS,
        cost_estimate=pl.CostEstimate(
            flops=2 * ROWS * D * KERNEL * 16, bytes_accessed=14 * 2**20, transcendentals=0
        ),
        name="mix",
    )(gated, taps, weights)


def down_kernel(mixed, before, behind, after, taps, gain, w, out, wide, head, tail):
    wide[...] = mixed[...]
    head[0:16, :] = before[...].astype(F32)
    head[16:32, :] = jnp.zeros((16, D), F32)
    tail[0:16, :] = jnp.zeros((16, D), F32)
    tail[16:32, :] = behind[...].astype(F32)
    for n in range(D // 128):
        cols = slice(n * 128, (n + 1) * 128)
        top = wide[0:16, cols]
        for k in range(15):
            top = top + head[k + 1 : k + 17, cols] * taps[k : k + 1, cols]
        wide[0:16, cols] = top
        bottom = wide[ROWS - 16 : ROWS, cols]
        for k in range(16, KERNEL):
            bottom = bottom + tail[k - 15 : k + 1, cols] * taps[k : k + 1, cols]
        wide[ROWS - 16 : ROWS, cols] = bottom
    normed = layer_norm(wide[...], gain[...])
    activated = (normed / (1.0 + jnp.exp(-normed))).astype(BF16)
    term = jnp.dot(activated, w[...], preferred_element_type=F32)
    out[...] = (after[...] + term).astype(BF16)


def down(mixed, before, behind, after, taps, gain, w):
    return pl.pallas_call(
        down_kernel,
        in_specs=[VMEM] * 7,
        out_specs=VMEM,
        out_shape=jax.ShapeDtypeStruct((ROWS, D), BF16),
        scratch_shapes=[
            pltpu.VMEM((ROWS, D), F32),
            pltpu.VMEM((32, D), F32),
            pltpu.VMEM((32, D), F32),
        ],
        compiler_params=PARAMS,
        cost_estimate=pl.CostEstimate(
            flops=2 * ROWS * D * D, bytes_accessed=8 * 2**20, transcendentals=ROWS * D
        ),
        name="down",
    )(mixed, before, behind, after, taps, gain, w)


def on_device(
    frames,
    frame_mask,
    attend_gain,
    w_query,
    w_key,
    w_value,
    w_out,
    conv_gain,
    w_expand,
    depth_kernel,
    depth_gain,
    w_down,
):
    own_frames = frames[0]

    top, bottom, heads, others = prepare(
        own_frames, frame_mask, attend_gain[None], w_query, w_key, w_value, w_out, w_expand, w_down
    )

    heads = lax.all_to_all(heads, ("x", "y"), split_axis=0, concat_axis=0, tiled=True)
    counts = heads[:, 0, HD].astype(jnp.int32)

    others, heads = lax.optimization_barrier((others, heads))
    weights = lax.all_gather(others, ("x", "y", "c", "z"), axis=0)

    top, heads = lax.optimization_barrier((top, heads))
    line0, line1 = gathered(top, "x"), gathered(bottom, "y")
    early = plane(line0, "y") + plane(line1, "x")
    own_w = jnp.stack(gathered(heads, "z"))
    early, own_w = lax.optimization_barrier((early, own_w))
    other_w = pull(own_w, "c", 1)

    q1, kv1, w, *passed = project_early(counts, early, own_w, other_w)
    late = [pull(p, a, j) for p, a, j in zip(passed, ("y", "y", "x", "x"), (1, 3, 1, 3))]
    kv1_other = pull(kv1, "c", 1)
    sums = attend_early(q1, kv1, kv1_other)
    w, sums = lax.optimization_barrier((w, sums))
    q2, kv2 = project_late(counts, late, w)
    kv2_other = pull(kv2, "c", 1)
    attended = attend_late(q1, q2, kv1, kv1_other, kv2, kv2_other, sums)
    attended = attended.reshape(16, ROWS, 128)
    attended = lax.all_to_all(attended, ("x", "y"), split_axis=0, concat_axis=0, tiled=True)

    after, gated = expand(frame_mask, attended, own_frames, conv_gain[None], weights)
    line = ("x", "y", "c")
    before = lax.ppermute(gated[ROWS - 16 :], line, [(i, i + 1) for i in range(31)])
    behind = lax.ppermute(gated[:16], line, [(i + 1, i) for i in range(31)])
    mixed, w_last = mix(gated, depth_kernel, weights)
    out = down(mixed, before, behind, after, depth_kernel, depth_gain[None], w_last)
    return out[None]


def solution(mesh):
    cells = Mesh(mesh.devices.reshape(4, 4, 2, 4), ("x", "y", "c", "z"))
    seq = ("x", "y", "c")
    spread = P(("x", "y", "c", "z"), None)
    in_specs = (
        P("z", seq, None),
        P("z", seq),
        P(),
        spread,
        spread,
        spread,
        spread,
        P(),
        spread,
        P(),
        P(),
        spread,
    )
    return jax.shard_map(
        on_device, mesh=cells, in_specs=in_specs, out_specs=P("z", seq, None), check_vma=False
    )
```

```python
import functools
import math

import jax
import jax.numpy as jnp
from jax import lax
from jax.experimental import pallas as pl
from jax.experimental.pallas import tpu as pltpu
from jax.sharding import Mesh, PartitionSpec as P

D = 1536
ROWS = 192
HD = 96
KERNEL = 31
FULL = 144
PART = 96
EARLY = 24 * PART
LATE = 8 * PART
BQ = EARLY // 2
BK = 384
SCALE = math.log2(math.e) / math.sqrt(HD)
NEG = -1e30
F32 = jnp.float32
BF16 = jnp.bfloat16
VMEM = pl.BlockSpec(memory_space=pltpu.VMEM)
SMEM = pl.BlockSpec(memory_space=pltpu.SMEM)
HBM = pl.BlockSpec(memory_space=pl.ANY)


def params(mib):
    return pltpu.CompilerParams(vmem_limit_bytes=mib * 2**20)


def pull(value, axis, step):
    count = lax.axis_size(axis)
    return lax.ppermute(value, axis, [((i + step) % count, i) for i in range(count)])


def gathered(value, axis):
    return [value] + [pull(value, axis, j) for j in (1, 2, 3)]


def plane(line, outer):
    line = jnp.stack(line)
    return [line, pull(line, outer, 1), pull(line, outer, 3)]


def parts():
    early = [
        (0, i, o) if side == 0 else (1, o, i)
        for side in range(2)
        for o in (0, 1, 3)
        for i in range(4)
    ]
    return early + [(0, i, 2) for i in range(4)] + [(1, 2, i) for i in range(4)]


def where_part(part):
    side, across, along = parts()[part]
    x, y = lax.axis_index("x"), lax.axis_index("y")
    return (x + across) % 4 * 4 + (y + along) % 4, side


def layer_norm(values, gain):
    center = values - jnp.mean(values, axis=-1, keepdims=True)
    spread = jnp.mean(center * center, axis=-1, keepdims=True)
    return center * lax.rsqrt(spread + 1e-05) * gain


def prepare_kernel(
    frames, mask, gain, wq, wk, wv, wo, we, wd, top, bottom, heads, others
):
    normed = layer_norm(frames[...].astype(F32), gain[...].reshape(1, D)).astype(BF16)
    top[...] = normed[:PART]
    bottom[...] = normed[PART:]
    count = jnp.sum(mask[...].astype(F32))
    lane = lax.broadcasted_iota(jnp.int32, (12, 128), 1)
    fill = jnp.where(lane == HD, count, 0.0).astype(BF16)
    heads[...] = jnp.zeros(heads.shape, BF16)
    for m, w in enumerate((wq, wk, wv)):
        for h in range(16):
            part = jnp.concatenate([w[:, h * HD : (h + 1) * HD], fill[:, HD:]], axis=1)
            heads[h, 0:12, m * 128 : (m + 1) * 128] = part
    others[...] = jnp.concatenate([wo[...], we[:, 0:D], we[:, D : 2 * D], wd[...]], axis=0)


def prepare(frames, mask, gain, wq, wk, wv, wo, we, wd):
    return pl.pallas_call(
        prepare_kernel,
        in_specs=[VMEM] * 9,
        out_specs=(VMEM,) * 4,
        out_shape=(
            jax.ShapeDtypeStruct((PART, D), BF16),
            jax.ShapeDtypeStruct((PART, D), BF16),
            jax.ShapeDtypeStruct((16, 16, 384), BF16),
            jax.ShapeDtypeStruct((48, D), BF16),
        ),
        compiler_params=params(56),
        name="prepare",
    )(frames, mask, gain, wq, wk, wv, wo, we, wd)


def project_rows(first, counts, rows, w, q_out, kv_out):
    n = rows.shape[0]
    lane = lax.broadcasted_iota(jnp.int32, (PART, 128), 1)
    row = lax.broadcasted_iota(jnp.int32, (PART, 128), 0)
    product = jnp.dot(rows.reshape(n * PART, D), w, preferred_element_type=F32)
    for j in range(n):
        part = product[j * PART : (j + 1) * PART]
        chunk, side = where_part(first + j)
        bias = jnp.where(row < counts[chunk] - side * PART, 0.0, NEG)
        span = slice((first + j) % 24 * PART, ((first + j) % 24 + 1) * PART)
        q_out[span, :] = jnp.where(lane == HD, 1.0, part[:, 0:128]).astype(BF16)
        kv_out[span, 0:128] = jnp.where(lane == HD, bias, part[:, 128:256]).astype(BF16)
        kv_out[span, 128:256] = jnp.where(lane == HD, 1.0, part[:, 256:384]).astype(BF16)


def early_kernel(counts, *refs):
    pieces, (own_w, other_w, q_out, kv_out, w_out), passed = refs[:6], refs[6:11], refs[11:15]
    rows, held, sems = refs[15:]
    c, z = lax.axis_index("c"), lax.axis_index("z")
    w_copies = [
        pltpu.make_async_copy(own_w, held.at[c], sems.at[6]),
        pltpu.make_async_copy(other_w, held.at[1 - c], sems.at[7]),
    ]
    for copy in w_copies:
        copy.start()
    copies = []
    for p in range(6):
        copies.append(
            pltpu.make_async_copy(pieces[p], rows.at[4 * p : 4 * p + 4], sems.at[p])
        )
        copies[-1].start()
    for copy in w_copies:
        copy.wait()
    for chunk in range(16):
        for core in range(2):
            w_out[(chunk * 2 + core) * 48 : (chunk * 2 + core + 1) * 48, :] = jnp.concatenate(
                [
                    held[core, k ^ z, chunk, 0:12, :]
                    for k in range(4)
                ],
                axis=0,
            )
    onward = []
    for side in range(2):
        for p in range(3):
            copies[side * 3 + p].wait()
        for k, first in ((0, 4), (1, 10)):
            first = first + 12 * side
            onward.append(
                pltpu.make_async_copy(
                    rows.at[first : first + 2], passed[2 * side + k], sems.at[8 + 2 * side + k]
                )
            )
            onward[-1].start()
        project_rows(
            12 * side, counts, rows[12 * side : 12 * side + 12], w_out[...], q_out, kv_out
        )
    for copy in onward:
        copy.wait()


def project_early(counts, pieces, own_w, other_w):
    return pl.pallas_call(
        early_kernel,
        in_specs=[SMEM] + [HBM] * 8,
        out_specs=(VMEM, VMEM, VMEM, HBM, HBM, HBM, HBM),
        out_shape=(
            jax.ShapeDtypeStruct((EARLY, 128), BF16),
            jax.ShapeDtypeStruct((EARLY, 256), BF16),
            jax.ShapeDtypeStruct((D, 384), BF16),
        )
        + (jax.ShapeDtypeStruct((2, PART, D), BF16),) * 4,
        scratch_shapes=[
            pltpu.VMEM((24, PART, D), BF16),
            pltpu.VMEM((2, 4, 16, 16, 384), BF16),
            pltpu.SemaphoreType.DMA((12,)),
        ],
        compiler_params=params(20),
        cost_estimate=pl.CostEstimate(
            flops=EARLY * D * 128, bytes_accessed=2**20, transcendentals=0
        ),
        name="project_early",
    )(counts, *pieces, own_w, other_w)


def late_kernel(counts, p0, p1, p2, p3, w, q_out, kv_out, rows, sems):
    copies = [
        pltpu.make_async_copy(p, rows.at[2 * i : 2 * i + 2], sems.at[i])
        for i, p in enumerate((p0, p1, p2, p3))
    ]
    for copy in copies:
        copy.start()
    for copy in copies:
        copy.wait()
    project_rows(24, counts, rows[...], w[...], q_out, kv_out)


def project_late(counts, pieces, w):
    return pl.pallas_call(
        late_kernel,
        in_specs=[SMEM] + [HBM] * 4 + [VMEM],
        out_specs=(VMEM, VMEM),
        out_shape=(
            jax.ShapeDtypeStruct((LATE, 128), BF16),
            jax.ShapeDtypeStruct((LATE, 256), BF16),
        ),
        scratch_shapes=[pltpu.VMEM((8, PART, D), BF16), pltpu.SemaphoreType.DMA((4,))],
        compiler_params=params(12),
        cost_estimate=pl.CostEstimate(
            flops=2 * LATE * D * 512, bytes_accessed=4 * 2**20, transcendentals=0
        ),
        name="project_late",
    )(counts, *pieces, w)


def largest(rows):
    wide = rows.astype(F32)
    lane = lax.broadcasted_iota(jnp.int32, wide.shape, 1)
    square = jnp.where(lane < HD, wide * wide, 0.0).astype(BF16)
    sums = jnp.dot(square, jnp.ones((128, 128), BF16), preferred_element_type=F32)
    return jnp.max(jnp.max(sums.reshape(-1, 8, 128), axis=0)) * 1.02


def attend_block(q, sources, bounded, first, finish):
    rows = q.shape[0]
    def scores(ref, start):
        return lax.dot_general(
            q,
            ref[pl.ds(start, BK), 0:128],
            (((1,), (1,)), ((), ())),
            preferred_element_type=F32,
        )

    def start_values():
        if first is None:
            return jnp.full((rows, 1), -3e38, F32), jnp.zeros((rows, 128), F32)
        return first()

    @pl.when(bounded)
    def _():
        acc = start_values()[1]
        for ref in sources:
            for i in range(ref.shape[0] // BK):
                p = jnp.exp2(scores(ref, i * BK) * SCALE).astype(BF16)
                acc = acc + jnp.dot(
                    p, ref[pl.ds(i * BK, BK), 128:256], preferred_element_type=F32
                )
        finish(jnp.zeros((rows, 1), F32), acc)

    @pl.when(jnp.logical_not(bounded))
    def _():
        def body(ref, i, carry):
            peak, acc = carry
            start = pl.multiple_of(i * BK, BK)
            s = scores(ref, start) * SCALE
            higher = jnp.maximum(peak, jnp.max(s, axis=1, keepdims=True))
            p = jnp.exp2(s - higher).astype(BF16)
            acc = acc * jnp.exp2(peak - higher) + jnp.dot(
                p, ref[pl.ds(start, BK), 128:256], preferred_element_type=F32
            )
            return higher, acc

        carry = start_values()
        for ref in sources:
            carry = lax.fori_loop(
                0, ref.shape[0] // BK, functools.partial(body, ref), carry
            )
        finish(*carry)


def limit(q, norm):
    return largest(q) * norm <= 60.0 * 60.0 * HD


def attend_early_kernel(q_ref, own, other, o_ref, norm):
    @pl.when(pl.program_id(0) == 0)
    def _():
        norm[0] = jnp.maximum(largest(own[:, 0:128]), largest(other[:, 0:128]))

    def finish(shift, acc):
        lane = lax.broadcasted_iota(jnp.int32, (BQ, 128), 1)
        acc = jnp.where(lane == HD + 1, shift, acc)
        o_ref[...] = jnp.where(lane == HD + 2, norm[0], acc)

    q = q_ref[...]
    attend_block(q, (own, other), limit(q, norm[0]), None, finish)


def attend_early(q, own, other):
    whole = pl.BlockSpec((EARLY, 256), lambda i: (0, 0))
    return pl.pallas_call(
        attend_early_kernel,
        grid=(EARLY // BQ,),
        in_specs=[pl.BlockSpec((BQ, 128), lambda i: (i, 0)), whole, whole],
        out_specs=pl.BlockSpec((BQ, 128), lambda i: (i, 0)),
        out_shape=jax.ShapeDtypeStruct((EARLY, 128), F32),
        scratch_shapes=[pltpu.SMEM((1,), F32)],
        compiler_params=params(28),
        cost_estimate=pl.CostEstimate(
            flops=EARLY * EARLY * 256, bytes_accessed=5 * 2**20, transcendentals=0
        ),
        name="attend_early",
    )(q, own, other)


def attend_late_kernel(
    table, q1, q2, own1, other1, own2, other2, sums, packed, norm, o_ref
):
    block = pl.program_id(0)
    x, y = lax.axis_index("x"), lax.axis_index("y")

    @pl.when(block == 0)
    def _():
        now = jnp.maximum(largest(own2[:, 0:128]), largest(other2[:, 0:128]))
        norm[0] = jnp.maximum(now, jnp.max(sums[0:8, HD + 2 : HD + 3]))

    def finish(shift, acc):
        out = (acc * (1.0 / acc[:, HD : HD + 1])).astype(BF16)
        for t in range(acc.shape[0] // PART):
            part = block * (BQ // PART) + t
            chunk = (x + table[1, part]) % 4 * 4 + (y + table[2, part]) % 4
            spot = pl.multiple_of(chunk * ROWS + table[0, part] * PART, PART)
            o_ref[pl.ds(spot, PART), :] = out[t * PART : (t + 1) * PART]

    @pl.when(block < EARLY // BQ)
    def _():
        q = q1[...]
        shift = sums[:, HD + 1 : HD + 2]
        settled = jnp.max(jnp.abs(shift)) == 0.0
        attend_block(
            q,
            (own2, other2),
            jnp.logical_and(limit(q, norm[0]), settled),
            lambda: (shift, sums[...]),
            finish,
        )

    @pl.when(block == EARLY // BQ)
    def _():
        q = q2[...]
        attend_block(q, (own1, other1, own2, other2), limit(q, norm[0]), None, finish)

        for chunk in range(16):
            rows = o_ref[chunk * ROWS : (chunk + 1) * ROWS, :]
            rest = [rows[FULL:, 32 * i : 32 * i + 32] for i in range(3)]
            packed[chunk] = jnp.concatenate(
                [rows[:FULL, 0:HD], jnp.concatenate(rest, axis=0)], axis=1
            )


def attend_late(q1, q2, own1, other1, own2, other2, sums):
    last = EARLY // BQ - 1

    def whole(rows, width):
        return pl.BlockSpec((rows, width), lambda i: (0, 0))

    def block(width):
        return pl.BlockSpec((BQ, width), lambda i: (jnp.minimum(i, last), 0))

    total = EARLY + LATE
    return pl.pallas_call(
        attend_late_kernel,
        grid=(EARLY // BQ + 1,),
        in_specs=[
            SMEM,
            block(128),
            whole(LATE, 128),
            whole(EARLY, 256),
            whole(EARLY, 256),
            whole(LATE, 256),
            whole(LATE, 256),
            block(128),
        ],
        out_specs=pl.BlockSpec((16, FULL, 128), lambda i: (0, 0, 0)),
        out_shape=jax.ShapeDtypeStruct((16, FULL, 128), BF16),
        scratch_shapes=[pltpu.SMEM((1,), F32), pltpu.VMEM((total, 128), BF16)],
        compiler_params=params(28),
        cost_estimate=pl.CostEstimate(
            flops=8 * (total * total - EARLY * EARLY) * 256,
            bytes_accessed=7 * 2**20,
            transcendentals=0,
        ),
        name="attend_late",
    )(jnp.array(parts(), jnp.int32).T, q1, q2, own1, other1, own2, other2, sums)


def unpack(target, tiles, k):
    low, high = 12 * k, 12 * k + 12
    for s in range(32):
        parts = []
        for i in range(4):
            for t in range(low // 16, (high - 1) // 16 + 1):
                a, b = max(low - 16 * t, 0), min(high - 16 * t, 16)
                parts.append(tiles[t][4 * s + i, a:b, :])
        target[48 * s : 48 * s + 48, :] = jnp.concatenate(parts, axis=0)


def expand_kernel(
    mask,
    att,
    frames,
    gain,
    weights,
    after_out,
    gated_out,
    head_out,
    tail_out,
    rows,
    t0,
    t1,
    t2,
    w,
    w2,
    sems,
):
    tiles = (t0, t1, t2)
    copies = [
        pltpu.make_async_copy(weights.at[:, 16 * t : 16 * t + 16, :], tiles[t], sems.at[t])
        for t in range(3)
    ]
    for copy in copies:
        copy.start()
    for h in range(16):
        rows[0:FULL, h * HD : (h + 1) * HD] = att[h, :, 0:HD]
        for i in range(3):
            cols = slice(h * HD + 32 * i, h * HD + 32 * i + 32)
            rows[FULL:ROWS, cols] = att[h, 48 * i : 48 * i + 48, HD:128]
    copies[0].wait()
    unpack(w, tiles, 0)
    out_term = jnp.dot(rows[...], w[...], preferred_element_type=F32)
    after = frames[...].astype(F32) + out_term
    after_out[...] = after
    normed = layer_norm(after, gain[...].reshape(1, D)).astype(BF16)
    copies[1].wait()
    unpack(w2, tiles, 1)
    copies[2].wait()
    unpack(w, tiles, 2)
    count = jnp.sum(mask[...].astype(F32))
    real = lax.broadcasted_iota(jnp.int32, (ROWS, 1), 0).astype(F32) < count
    for n in range(3):
        cols = slice(n * 512, (n + 1) * 512)
        left = jnp.dot(normed, w2[:, cols], preferred_element_type=F32)
        right = jnp.dot(normed, w[:, cols], preferred_element_type=F32)
        gate = left * (1.0 / (1.0 + jnp.exp(-right)))
        gated = jnp.where(real, gate, 0.0).astype(BF16)
        gated_out[:, cols] = gated
        head_out[:, cols] = gated[0:16]
        tail_out[:, cols] = gated[ROWS - 16 : ROWS]


def expand(mask, att, frames, gain, weights):
    return pl.pallas_call(
        expand_kernel,
        in_specs=[VMEM, VMEM, VMEM, VMEM, HBM],
        out_specs=(VMEM,) * 4,
        out_shape=(
            jax.ShapeDtypeStruct((ROWS, D), F32),
            jax.ShapeDtypeStruct((ROWS, D), BF16),
            jax.ShapeDtypeStruct((16, D), BF16),
            jax.ShapeDtypeStruct((16, D), BF16),
        ),
        scratch_shapes=[pltpu.VMEM((ROWS, D), BF16)]
        + [pltpu.VMEM((128, 16, D), BF16)] * 3
        + [pltpu.VMEM((D, D), BF16)] * 2
        + [pltpu.SemaphoreType.DMA((3,))],
        compiler_params=params(44),
        cost_estimate=pl.CostEstimate(
            flops=2 * ROWS * D * D * 3, bytes_accessed=20 * 2**20, transcendentals=ROWS * D
        ),
        name="expand",
    )(mask, att, frames, gain, weights)


def mix_kernel(gated, taps, mixed, wide):
    wide[0:16, :] = jnp.zeros((16, D), F32)
    wide[16 : 16 + ROWS, :] = gated[...].astype(F32)
    wide[16 + ROWS : 32 + ROWS, :] = jnp.zeros((16, D), F32)
    for n in range(D // 128):
        cols = slice(n * 128, (n + 1) * 128)
        acc = jnp.zeros((ROWS, 128), F32)
        for s in range(8):
            shifted = wide[s : s + ROWS + 24, cols]
            for a in range(4):
                k = 8 * a + s - 1
                if 0 <= k < KERNEL:
                    acc = acc + shifted[8 * a : 8 * a + ROWS] * taps[k : k + 1, cols]
        mixed[:, cols] = acc


def mix(gated, taps):
    return pl.pallas_call(
        mix_kernel,
        in_specs=[VMEM, VMEM],
        out_specs=VMEM,
        out_shape=jax.ShapeDtypeStruct((ROWS, D), F32),
        scratch_shapes=[pltpu.VMEM((ROWS + 32, D), F32)],
        compiler_params=params(16),
        cost_estimate=pl.CostEstimate(
            flops=2 * ROWS * D * KERNEL * 16, bytes_accessed=14 * 2**20, transcendentals=0
        ),
        name="mix",
    )(gated, taps)


def down_kernel(
    mixed, before, behind, after, taps, gain, weights, out, wide, head, tail, tile, w, sem
):
    copy = pltpu.make_async_copy(weights.at[:, 32:48, :], tile, sem)
    copy.start()
    wide[...] = mixed[...]
    head[0:16, :] = before[...].astype(F32)
    head[16:32, :] = jnp.zeros((16, D), F32)
    tail[0:16, :] = jnp.zeros((16, D), F32)
    tail[16:32, :] = behind[...].astype(F32)
    for n in range(D // 128):
        cols = slice(n * 128, (n + 1) * 128)
        top = wide[0:16, cols]
        for k in range(15):
            top = top + head[k + 1 : k + 17, cols] * taps[k : k + 1, cols]
        wide[0:16, cols] = top
        bottom = wide[ROWS - 16 : ROWS, cols]
        for k in range(16, KERNEL):
            bottom = bottom + tail[k - 15 : k + 1, cols] * taps[k : k + 1, cols]
        wide[ROWS - 16 : ROWS, cols] = bottom
    normed = layer_norm(wide[...], gain[...].reshape(1, D))
    activated = (normed / (1.0 + jnp.exp(-normed))).astype(BF16)
    copy.wait()
    unpack(w, (None, None, tile), 3)
    term = jnp.dot(activated, w[...], preferred_element_type=F32)
    out[...] = (after[...] + term).astype(BF16)


def down(mixed, before, behind, after, taps, gain, weights):
    return pl.pallas_call(
        down_kernel,
        in_specs=[VMEM] * 6 + [HBM],
        out_specs=VMEM,
        out_shape=jax.ShapeDtypeStruct((ROWS, D), BF16),
        scratch_shapes=[
            pltpu.VMEM((ROWS, D), F32),
            pltpu.VMEM((32, D), F32),
            pltpu.VMEM((32, D), F32),
            pltpu.VMEM((128, 16, D), BF16),
            pltpu.VMEM((D, D), BF16),
            pltpu.SemaphoreType.DMA,
        ],
        compiler_params=params(48),
        cost_estimate=pl.CostEstimate(
            flops=2 * ROWS * D * D, bytes_accessed=8 * 2**20, transcendentals=ROWS * D
        ),
        name="down",
    )(mixed, before, behind, after, taps, gain, weights)


def on_device(
    frames,
    frame_mask,
    attend_gain,
    w_query,
    w_key,
    w_value,
    w_out,
    conv_gain,
    w_expand,
    depth_kernel,
    depth_gain,
    w_down,
):
    own_frames = frames[0]

    top, bottom, heads, others = prepare(
        own_frames, frame_mask, attend_gain, w_query, w_key, w_value, w_out, w_expand, w_down
    )

    heads = lax.all_to_all(heads, ("x", "y"), split_axis=0, concat_axis=0, tiled=True)
    counts = heads[:, 0, HD].astype(jnp.int32)

    others, heads = lax.optimization_barrier((others, heads))
    weights = lax.all_gather(others, ("x", "y", "c", "z"), axis=0)

    line0, line1 = gathered(top, "x"), gathered(bottom, "y")
    early = plane(line0, "y") + plane(line1, "x")
    swap = [[(i, i ^ k) for i in range(4)] for k in (1, 2)]
    own_w = jnp.stack([heads, lax.ppermute(heads, "z", swap[0])])
    own_w = jnp.concatenate([own_w, lax.ppermute(own_w, "z", swap[1])])
    early, own_w = lax.optimization_barrier((early, own_w))
    other_w = pull(own_w, "c", 1)

    q1, kv1, w, *passed = project_early(counts, early, own_w, other_w)
    late = [pull(p, a, j) for p, a, j in zip(passed, ("y", "y", "x", "x"), (1, 3, 1, 3))]
    kv1_other = pull(kv1, "c", 1)
    sums = attend_early(q1, kv1, kv1_other)
    w, sums = lax.optimization_barrier((w, sums))
    q2, kv2 = project_late(counts, late, w)
    kv2_other = pull(kv2, "c", 1)
    attended = attend_late(q1, q2, kv1, kv1_other, kv2, kv2_other, sums)
    attended = lax.all_to_all(attended, ("x", "y"), split_axis=0, concat_axis=0, tiled=True)

    after, gated, head, tail = expand(frame_mask, attended, own_frames, conv_gain, weights)
    line = ("x", "y", "c")
    before = lax.ppermute(tail, line, [(i, i + 1) for i in range(31)])
    behind = lax.ppermute(head, line, [(i + 1, i) for i in range(31)])
    mixed = mix(gated, depth_kernel)
    out = down(mixed, before, behind, after, depth_kernel, depth_gain, weights)
    return out[None]


def solution(mesh):
    cells = Mesh(mesh.devices.reshape(4, 4, 2, 4), ("x", "y", "c", "z"))
    seq = ("x", "y", "c")
    spread = P(("x", "y", "c", "z"), None)
    in_specs = (
        P("z", seq, None),
        P("z", seq),
        P(),
        spread,
        spread,
        spread,
        spread,
        P(),
        spread,
        P(),
        P(),
        spread,
    )
    return jax.shard_map(
        on_device, mesh=cells, in_specs=in_specs, out_specs=P("z", seq, None), check_vma=False
    )
```

```python
import functools
import math

import jax
import jax.numpy as jnp
from jax import lax
from jax.experimental import pallas as pl
from jax.experimental.pallas import tpu as pltpu
from jax.sharding import Mesh, PartitionSpec as P

D = 1536
ROWS = 192
HD = 96
KERNEL = 31
FULL = 144
PART = 96
EARLY = 24 * PART
LATE = 8 * PART
BQ = EARLY // 2
BK = 384
SCALE = math.log2(math.e) / math.sqrt(HD)
NEG = -1e30
F32 = jnp.float32
BF16 = jnp.bfloat16
VMEM = pl.BlockSpec(memory_space=pltpu.VMEM)
SMEM = pl.BlockSpec(memory_space=pltpu.SMEM)
HBM = pl.BlockSpec(memory_space=pl.ANY)


def params(mib):
    return pltpu.CompilerParams(vmem_limit_bytes=mib * 2**20)


def pull(value, axis, step):
    count = lax.axis_size(axis)
    return lax.ppermute(value, axis, [((i + step) % count, i) for i in range(count)])


def gathered(value, axis):
    return [value] + [pull(value, axis, j) for j in (1, 2, 3)]


def plane(line, outer):
    line = jnp.stack(line)
    return [line, pull(line, outer, 1), pull(line, outer, 3)]


def parts():
    early = [
        (0, i, o) if side == 0 else (1, o, i)
        for side in range(2)
        for o in (0, 1, 3)
        for i in range(4)
    ]
    return early + [(0, i, 2) for i in range(4)] + [(1, 2, i) for i in range(4)]


def where_part(part):
    side, across, along = parts()[part]
    x, y = lax.axis_index("x"), lax.axis_index("y")
    return (x + across) % 4 * 4 + (y + along) % 4, side


def layer_norm(values, gain):
    center = values - jnp.mean(values, axis=-1, keepdims=True)
    spread = jnp.mean(center * center, axis=-1, keepdims=True)
    return center * lax.rsqrt(spread + 1e-05) * gain


def prepare_kernel(
    frames, mask, gain, wq, wk, wv, wo, we, wd, top, bottom, heads, others
):
    normed = layer_norm(frames[...].astype(F32), gain[...].reshape(1, D)).astype(BF16)
    top[...] = normed[:PART]
    bottom[...] = normed[PART:]
    count = jnp.sum(mask[...].astype(F32))
    lane = lax.broadcasted_iota(jnp.int32, (12, 128), 1)
    fill = jnp.where(lane == HD, count, 0.0).astype(BF16)
    heads[...] = jnp.zeros(heads.shape, BF16)
    for m, w in enumerate((wq, wk, wv)):
        for h in range(16):
            part = jnp.concatenate([w[:, h * HD : (h + 1) * HD], fill[:, HD:]], axis=1)
            heads[h, 0:12, m * 128 : (m + 1) * 128] = part
    others[...] = jnp.concatenate([wo[...], we[:, 0:D], we[:, D : 2 * D], wd[...]], axis=0)


def prepare(frames, mask, gain, wq, wk, wv, wo, we, wd):
    return pl.pallas_call(
        prepare_kernel,
        in_specs=[VMEM] * 9,
        out_specs=(VMEM,) * 4,
        out_shape=(
            jax.ShapeDtypeStruct((PART, D), BF16),
            jax.ShapeDtypeStruct((PART, D), BF16),
            jax.ShapeDtypeStruct((16, 16, 384), BF16),
            jax.ShapeDtypeStruct((48, D), BF16),
        ),
        compiler_params=params(56),
        name="prepare",
    )(frames, mask, gain, wq, wk, wv, wo, we, wd)


def project_rows(first, counts, rows, w, q_out, kv_out):
    n = rows.shape[0]
    lane = lax.broadcasted_iota(jnp.int32, (PART, 128), 1)
    row = lax.broadcasted_iota(jnp.int32, (PART, 128), 0)
    product = jnp.dot(rows.reshape(n * PART, D), w, preferred_element_type=F32)
    for j in range(n):
        part = product[j * PART : (j + 1) * PART]
        chunk, side = where_part(first + j)
        bias = jnp.where(row < counts[chunk] - side * PART, 0.0, NEG)
        span = slice((first + j) % 24 * PART, ((first + j) % 24 + 1) * PART)
        q_out[span, :] = jnp.where(lane == HD, 1.0, part[:, 0:128]).astype(BF16)
        kv_out[span, 0:128] = jnp.where(lane == HD, bias, part[:, 128:256]).astype(BF16)
        kv_out[span, 128:256] = jnp.where(lane == HD, 1.0, part[:, 256:384]).astype(BF16)


def early_kernel(counts, *refs):
    pieces, (own_w, other_w, q_out, kv_out, w_out), passed = refs[:6], refs[6:11], refs[11:15]
    rows, held, sems = refs[15:]
    c, z = lax.axis_index("c"), lax.axis_index("z")
    w_copies = [
        pltpu.make_async_copy(own_w, held.at[c], sems.at[6]),
        pltpu.make_async_copy(other_w, held.at[1 - c], sems.at[7]),
    ]
    for copy in w_copies:
        copy.start()
    copies = []
    for p in range(6):
        copies.append(
            pltpu.make_async_copy(pieces[p], rows.at[4 * p : 4 * p + 4], sems.at[p])
        )
        copies[-1].start()
    for copy in w_copies:
        copy.wait()
    for chunk in range(16):
        for core in range(2):
            w_out[(chunk * 2 + core) * 48 : (chunk * 2 + core + 1) * 48, :] = jnp.concatenate(
                [
                    held[core, k ^ z, chunk, 0:12, :]
                    for k in range(4)
                ],
                axis=0,
            )
    onward = []
    for side in range(2):
        for p in range(3):
            copies[side * 3 + p].wait()
        for k, first in ((0, 4), (1, 10)):
            first = first + 12 * side
            onward.append(
                pltpu.make_async_copy(
                    rows.at[first : first + 2], passed[2 * side + k], sems.at[8 + 2 * side + k]
                )
            )
            onward[-1].start()
        project_rows(
            12 * side, counts, rows[12 * side : 12 * side + 12], w_out[...], q_out, kv_out
        )
    for copy in onward:
        copy.wait()


def project_early(counts, pieces, own_w, other_w):
    return pl.pallas_call(
        early_kernel,
        in_specs=[SMEM] + [HBM] * 8,
        out_specs=(VMEM, VMEM, VMEM, HBM, HBM, HBM, HBM),
        out_shape=(
            jax.ShapeDtypeStruct((EARLY, 128), BF16),
            jax.ShapeDtypeStruct((EARLY, 256), BF16),
            jax.ShapeDtypeStruct((D, 384), BF16),
        )
        + (jax.ShapeDtypeStruct((2, PART, D), BF16),) * 4,
        scratch_shapes=[
            pltpu.VMEM((24, PART, D), BF16),
            pltpu.VMEM((2, 4, 16, 16, 384), BF16),
            pltpu.SemaphoreType.DMA((12,)),
        ],
        compiler_params=params(20),
        cost_estimate=pl.CostEstimate(
            flops=EARLY * D * 128, bytes_accessed=2**20, transcendentals=0
        ),
        name="project_early",
    )(counts, *pieces, own_w, other_w)


def late_kernel(counts, p0, p1, p2, p3, w, q_out, kv_out, rows, sems):
    copies = [
        pltpu.make_async_copy(p, rows.at[2 * i : 2 * i + 2], sems.at[i])
        for i, p in enumerate((p0, p1, p2, p3))
    ]
    for copy in copies:
        copy.start()
    for copy in copies:
        copy.wait()
    project_rows(24, counts, rows[...], w[...], q_out, kv_out)


def project_late(counts, pieces, w):
    return pl.pallas_call(
        late_kernel,
        in_specs=[SMEM] + [HBM] * 4 + [VMEM],
        out_specs=(VMEM, VMEM),
        out_shape=(
            jax.ShapeDtypeStruct((LATE, 128), BF16),
            jax.ShapeDtypeStruct((LATE, 256), BF16),
        ),
        scratch_shapes=[pltpu.VMEM((8, PART, D), BF16), pltpu.SemaphoreType.DMA((4,))],
        compiler_params=params(12),
        cost_estimate=pl.CostEstimate(
            flops=2 * LATE * D * 512, bytes_accessed=4 * 2**20, transcendentals=0
        ),
        name="project_late",
    )(counts, *pieces, w)


def largest(rows):
    wide = rows.astype(F32)
    lane = lax.broadcasted_iota(jnp.int32, wide.shape, 1)
    square = jnp.where(lane < HD, wide * wide, 0.0).astype(BF16)
    sums = jnp.dot(square, jnp.ones((128, 128), BF16), preferred_element_type=F32)
    return jnp.max(jnp.max(sums.reshape(-1, 8, 128), axis=0)) * 1.02


def attend_block(q, sources, bounded, first, finish):
    rows = q.shape[0]
    def scores(ref, start):
        return lax.dot_general(
            q,
            ref[pl.ds(start, BK), 0:128],
            (((1,), (1,)), ((), ())),
            preferred_element_type=F32,
        )

    def start_values():
        if first is None:
            return jnp.full((rows, 1), -3e38, F32), jnp.zeros((rows, 128), F32)
        return first()

    @pl.when(bounded)
    def _():
        acc = start_values()[1]
        for ref in sources:
            for i in range(ref.shape[0] // BK):
                p = jnp.exp2(scores(ref, i * BK) * SCALE).astype(BF16)
                acc = acc + jnp.dot(
                    p, ref[pl.ds(i * BK, BK), 128:256], preferred_element_type=F32
                )
        finish(jnp.zeros((rows, 1), F32), acc)

    @pl.when(jnp.logical_not(bounded))
    def _():
        def body(ref, i, carry):
            peak, acc = carry
            start = pl.multiple_of(i * BK, BK)
            s = scores(ref, start) * SCALE
            higher = jnp.maximum(peak, jnp.max(s, axis=1, keepdims=True))
            p = jnp.exp2(s - higher).astype(BF16)
            acc = acc * jnp.exp2(peak - higher) + jnp.dot(
                p, ref[pl.ds(start, BK), 128:256], preferred_element_type=F32
            )
            return higher, acc

        carry = start_values()
        for ref in sources:
            carry = lax.fori_loop(
                0, ref.shape[0] // BK, functools.partial(body, ref), carry
            )
        finish(*carry)


def limit(q, norm):
    return largest(q) * norm <= 60.0 * 60.0 * HD


def attend_early_kernel(q_ref, own, other, o_ref, norm):
    @pl.when(pl.program_id(0) == 0)
    def _():
        norm[0] = jnp.maximum(largest(own[:, 0:128]), largest(other[:, 0:128]))

    def finish(shift, acc):
        lane = lax.broadcasted_iota(jnp.int32, (BQ, 128), 1)
        acc = jnp.where(lane == HD + 1, shift, acc)
        o_ref[...] = jnp.where(lane == HD + 2, norm[0], acc)

    q = q_ref[...]
    attend_block(q, (own, other), limit(q, norm[0]), None, finish)


def attend_early(q, own, other):
    whole = pl.BlockSpec((EARLY, 256), lambda i: (0, 0))
    return pl.pallas_call(
        attend_early_kernel,
        grid=(EARLY // BQ,),
        in_specs=[pl.BlockSpec((BQ, 128), lambda i: (i, 0)), whole, whole],
        out_specs=pl.BlockSpec((BQ, 128), lambda i: (i, 0)),
        out_shape=jax.ShapeDtypeStruct((EARLY, 128), F32),
        scratch_shapes=[pltpu.SMEM((1,), F32)],
        compiler_params=params(28),
        cost_estimate=pl.CostEstimate(
            flops=EARLY * EARLY * 256, bytes_accessed=5 * 2**20, transcendentals=0
        ),
        name="attend_early",
    )(q, own, other)


def attend_late_kernel(
    table, q1, q2, own1, other1, own2, other2, sums, packed, norm, o_ref
):
    block = pl.program_id(0)
    x, y = lax.axis_index("x"), lax.axis_index("y")

    @pl.when(block == 0)
    def _():
        now = jnp.maximum(largest(own2[:, 0:128]), largest(other2[:, 0:128]))
        norm[0] = jnp.maximum(now, jnp.max(sums[0:8, HD + 2 : HD + 3]))

    def finish(shift, acc):
        out = (acc * (1.0 / acc[:, HD : HD + 1])).astype(BF16)
        for t in range(acc.shape[0] // PART):
            part = block * (BQ // PART) + t
            chunk = (x + table[1, part]) % 4 * 4 + (y + table[2, part]) % 4
            spot = pl.multiple_of(chunk * ROWS + table[0, part] * PART, PART)
            o_ref[pl.ds(spot, PART), :] = out[t * PART : (t + 1) * PART]

    @pl.when(block < EARLY // BQ)
    def _():
        q = q1[...]
        shift = sums[:, HD + 1 : HD + 2]
        settled = jnp.max(jnp.abs(shift)) == 0.0
        attend_block(
            q,
            (own2, other2),
            jnp.logical_and(limit(q, norm[0]), settled),
            lambda: (shift, sums[...]),
            finish,
        )

    @pl.when(block == EARLY // BQ)
    def _():
        q = q2[...]
        attend_block(q, (own1, other1, own2, other2), limit(q, norm[0]), None, finish)

        for chunk in range(16):
            rows = o_ref[chunk * ROWS : (chunk + 1) * ROWS, :]
            rest = [rows[FULL:, 32 * i : 32 * i + 32] for i in range(3)]
            packed[chunk] = jnp.concatenate(
                [rows[:FULL, 0:HD], jnp.concatenate(rest, axis=0)], axis=1
            )


def attend_late(q1, q2, own1, other1, own2, other2, sums):
    last = EARLY // BQ - 1

    def whole(rows, width):
        return pl.BlockSpec((rows, width), lambda i: (0, 0))

    def block(width):
        return pl.BlockSpec((BQ, width), lambda i: (jnp.minimum(i, last), 0))

    total = EARLY + LATE
    return pl.pallas_call(
        attend_late_kernel,
        grid=(EARLY // BQ + 1,),
        in_specs=[
            SMEM,
            block(128),
            whole(LATE, 128),
            whole(EARLY, 256),
            whole(EARLY, 256),
            whole(LATE, 256),
            whole(LATE, 256),
            block(128),
        ],
        out_specs=pl.BlockSpec((16, FULL, 128), lambda i: (0, 0, 0)),
        out_shape=jax.ShapeDtypeStruct((16, FULL, 128), BF16),
        scratch_shapes=[pltpu.SMEM((1,), F32), pltpu.VMEM((total, 128), BF16)],
        compiler_params=params(28),
        cost_estimate=pl.CostEstimate(
            flops=8 * (total * total - EARLY * EARLY) * 256,
            bytes_accessed=7 * 2**20,
            transcendentals=0,
        ),
        name="attend_late",
    )(jnp.array(parts(), jnp.int32).T, q1, q2, own1, other1, own2, other2, sums)


def unpack(target, tiles, k):
    low, high = 12 * k, 12 * k + 12
    for s in range(32):
        parts = []
        for i in range(4):
            for t in range(low // 16, (high - 1) // 16 + 1):
                a, b = max(low - 16 * t, 0), min(high - 16 * t, 16)
                parts.append(tiles[t][4 * s + i, a:b, :])
        target[48 * s : 48 * s + 48, :] = jnp.concatenate(parts, axis=0)


def expand_kernel(
    mask,
    att,
    frames,
    gain,
    weights,
    after_out,
    gated_out,
    head_out,
    tail_out,
    rows,
    t0,
    t1,
    t2,
    w,
    w2,
    sems,
):
    tiles = (t0, t1, t2)
    copies = [
        pltpu.make_async_copy(weights.at[:, 16 * t : 16 * t + 16, :], tiles[t], sems.at[t])
        for t in range(3)
    ]
    for copy in copies:
        copy.start()
    for h in range(16):
        rows[0:FULL, h * HD : (h + 1) * HD] = att[h, :, 0:HD]
        for i in range(3):
            cols = slice(h * HD + 32 * i, h * HD + 32 * i + 32)
            rows[FULL:ROWS, cols] = att[h, 48 * i : 48 * i + 48, HD:128]
    copies[0].wait()
    unpack(w, tiles, 0)
    out_term = jnp.dot(rows[...], w[...], preferred_element_type=F32)
    after = frames[...].astype(F32) + out_term
    after_out[...] = after
    normed = layer_norm(after, gain[...].reshape(1, D)).astype(BF16)
    copies[1].wait()
    unpack(w2, tiles, 1)
    copies[2].wait()
    unpack(w, tiles, 2)
    count = jnp.sum(mask[...].astype(F32))
    real = lax.broadcasted_iota(jnp.int32, (ROWS, 1), 0).astype(F32) < count
    for n in range(3):
        cols = slice(n * 512, (n + 1) * 512)
        left = jnp.dot(normed, w2[:, cols], preferred_element_type=F32)
        right = jnp.dot(normed, w[:, cols], preferred_element_type=F32)
        gate = left * (1.0 / (1.0 + jnp.exp(-right)))
        gated = jnp.where(real, gate, 0.0).astype(BF16)
        gated_out[:, cols] = gated
        head_out[:, cols] = gated[0:16]
        tail_out[:, cols] = gated[ROWS - 16 : ROWS]


def expand(mask, att, frames, gain, weights):
    return pl.pallas_call(
        expand_kernel,
        in_specs=[VMEM, VMEM, VMEM, VMEM, HBM],
        out_specs=(VMEM,) * 4,
        out_shape=(
            jax.ShapeDtypeStruct((ROWS, D), F32),
            jax.ShapeDtypeStruct((ROWS, D), BF16),
            jax.ShapeDtypeStruct((16, D), BF16),
            jax.ShapeDtypeStruct((16, D), BF16),
        ),
        scratch_shapes=[pltpu.VMEM((ROWS, D), BF16)]
        + [pltpu.VMEM((128, 16, D), BF16)] * 3
        + [pltpu.VMEM((D, D), BF16)] * 2
        + [pltpu.SemaphoreType.DMA((3,))],
        compiler_params=params(44),
        cost_estimate=pl.CostEstimate(
            flops=2 * ROWS * D * D * 3, bytes_accessed=20 * 2**20, transcendentals=ROWS * D
        ),
        name="expand",
    )(mask, att, frames, gain, weights)


def mix_kernel(gated, taps, mixed, wide):
    wide[0:16, :] = jnp.zeros((16, D), F32)
    wide[16 : 16 + ROWS, :] = gated[...].astype(F32)
    wide[16 + ROWS : 32 + ROWS, :] = jnp.zeros((16, D), F32)
    for n in range(D // 128):
        cols = slice(n * 128, (n + 1) * 128)
        acc = jnp.zeros((ROWS, 128), F32)
        for s in range(8):
            shifted = wide[s : s + ROWS + 24, cols]
            for a in range(4):
                k = 8 * a + s - 1
                if 0 <= k < KERNEL:
                    acc = acc + shifted[8 * a : 8 * a + ROWS] * taps[k : k + 1, cols]
        mixed[:, cols] = acc


def mix(gated, taps):
    return pl.pallas_call(
        mix_kernel,
        in_specs=[VMEM, VMEM],
        out_specs=VMEM,
        out_shape=jax.ShapeDtypeStruct((ROWS, D), F32),
        scratch_shapes=[pltpu.VMEM((ROWS + 32, D), F32)],
        compiler_params=params(16),
        cost_estimate=pl.CostEstimate(
            flops=2 * ROWS * D * KERNEL * 16, bytes_accessed=14 * 2**20, transcendentals=0
        ),
        name="mix",
    )(gated, taps)


def down_kernel(
    mixed, before, behind, after, taps, gain, weights, out, wide, head, tail, tile, w, sem
):
    copy = pltpu.make_async_copy(weights.at[:, 32:48, :], tile, sem)
    copy.start()
    wide[...] = mixed[...]
    head[0:16, :] = before[...].astype(F32)
    head[16:32, :] = jnp.zeros((16, D), F32)
    tail[0:16, :] = jnp.zeros((16, D), F32)
    tail[16:32, :] = behind[...].astype(F32)
    for n in range(D // 128):
        cols = slice(n * 128, (n + 1) * 128)
        top = wide[0:16, cols]
        for k in range(15):
            top = top + head[k + 1 : k + 17, cols] * taps[k : k + 1, cols]
        wide[0:16, cols] = top
        bottom = wide[ROWS - 16 : ROWS, cols]
        for k in range(16, KERNEL):
            bottom = bottom + tail[k - 15 : k + 1, cols] * taps[k : k + 1, cols]
        wide[ROWS - 16 : ROWS, cols] = bottom
    normed = layer_norm(wide[...], gain[...].reshape(1, D))
    activated = (normed / (1.0 + jnp.exp(-normed))).astype(BF16)
    copy.wait()
    unpack(w, (None, None, tile), 3)
    term = jnp.dot(activated, w[...], preferred_element_type=F32)
    out[...] = (after[...] + term).astype(BF16)


def down(mixed, before, behind, after, taps, gain, weights):
    return pl.pallas_call(
        down_kernel,
        in_specs=[VMEM] * 6 + [HBM],
        out_specs=VMEM,
        out_shape=jax.ShapeDtypeStruct((ROWS, D), BF16),
        scratch_shapes=[
            pltpu.VMEM((ROWS, D), F32),
            pltpu.VMEM((32, D), F32),
            pltpu.VMEM((32, D), F32),
            pltpu.VMEM((128, 16, D), BF16),
            pltpu.VMEM((D, D), BF16),
            pltpu.SemaphoreType.DMA,
        ],
        compiler_params=params(48),
        cost_estimate=pl.CostEstimate(
            flops=2 * ROWS * D * D, bytes_accessed=8 * 2**20, transcendentals=ROWS * D
        ),
        name="down",
    )(mixed, before, behind, after, taps, gain, weights)


def on_device(
    frames,
    frame_mask,
    attend_gain,
    w_query,
    w_key,
    w_value,
    w_out,
    conv_gain,
    w_expand,
    depth_kernel,
    depth_gain,
    w_down,
):
    own_frames = frames[0]

    top, bottom, heads, others = prepare(
        own_frames, frame_mask, attend_gain, w_query, w_key, w_value, w_out, w_expand, w_down
    )

    weights = lax.all_gather(others, ("x", "y", "c", "z"), axis=0)

    line0, line1 = gathered(top, "x"), gathered(bottom, "y")

    heads, *_ = lax.optimization_barrier((heads, line1[1]))
    heads = lax.all_to_all(heads, ("x", "y"), split_axis=0, concat_axis=0, tiled=True)
    counts = heads[:, 0, HD].astype(jnp.int32)
    line0, line1, heads = lax.optimization_barrier((line0, line1, heads))
    early = plane(line0, "y") + plane(line1, "x")
    swap = [[(i, i ^ k) for i in range(4)] for k in (1, 2)]
    own_w = jnp.stack([heads, lax.ppermute(heads, "z", swap[0])])
    own_w = jnp.concatenate([own_w, lax.ppermute(own_w, "z", swap[1])])
    early, own_w = lax.optimization_barrier((early, own_w))
    other_w = pull(own_w, "c", 1)

    q1, kv1, w, *passed = project_early(counts, early, own_w, other_w)
    late = [pull(p, a, j) for p, a, j in zip(passed, ("y", "y", "x", "x"), (1, 3, 1, 3))]
    kv1_other = pull(kv1, "c", 1)
    sums = attend_early(q1, kv1, kv1_other)
    w, sums = lax.optimization_barrier((w, sums))
    q2, kv2 = project_late(counts, late, w)
    kv2_other = pull(kv2, "c", 1)
    attended = attend_late(q1, q2, kv1, kv1_other, kv2, kv2_other, sums)
    attended = lax.all_to_all(attended, ("x", "y"), split_axis=0, concat_axis=0, tiled=True)

    after, gated, head, tail = expand(frame_mask, attended, own_frames, conv_gain, weights)
    line = ("x", "y", "c")
    before = lax.ppermute(tail, line, [(i, i + 1) for i in range(31)])
    behind = lax.ppermute(head, line, [(i + 1, i) for i in range(31)])
    mixed = mix(gated, depth_kernel)
    out = down(mixed, before, behind, after, depth_kernel, depth_gain, weights)
    return out[None]


def solution(mesh):
    cells = Mesh(mesh.devices.reshape(4, 4, 2, 4), ("x", "y", "c", "z"))
    seq = ("x", "y", "c")
    spread = P(("x", "y", "c", "z"), None)
    in_specs = (
        P("z", seq, None),
        P("z", seq),
        P(),
        spread,
        spread,
        spread,
        spread,
        P(),
        spread,
        P(),
        P(),
        spread,
    )
    return jax.shard_map(
        on_device, mesh=cells, in_specs=in_specs, out_specs=P("z", seq, None), check_vma=False
    )
```

```python
import functools
import math

import jax
import jax.numpy as jnp
from jax import lax
from jax.experimental import pallas as pl
from jax.experimental.pallas import tpu as pltpu
from jax.sharding import Mesh, PartitionSpec as P

D = 1536
ROWS = 192
HD = 96
KERNEL = 31
FULL = 144
PART = 96
EARLY = 24 * PART
LATE = 8 * PART
BQ = EARLY // 2
BK = 384
SCALE = math.log2(math.e) / math.sqrt(HD)
NEG = -1e30
F32 = jnp.float32
BF16 = jnp.bfloat16
VMEM = pl.BlockSpec(memory_space=pltpu.VMEM)
SMEM = pl.BlockSpec(memory_space=pltpu.SMEM)
HBM = pl.BlockSpec(memory_space=pl.ANY)


def params(mib):
    return pltpu.CompilerParams(vmem_limit_bytes=mib * 2**20)


def pull(value, axis, step):
    count = lax.axis_size(axis)
    return lax.ppermute(value, axis, [((i + step) % count, i) for i in range(count)])


def gathered(value, axis):
    return [value] + [pull(value, axis, j) for j in (1, 2, 3)]


def plane(line, outer):
    line = jnp.stack(line)
    return [line, pull(line, outer, 1), pull(line, outer, 3)]


def parts():
    early = [
        (0, i, o) if side == 0 else (1, o, i)
        for side in range(2)
        for o in (0, 1, 3)
        for i in range(4)
    ]
    return early + [(0, i, 2) for i in range(4)] + [(1, 2, i) for i in range(4)]


def where_part(part):
    side, across, along = parts()[part]
    x, y = lax.axis_index("x"), lax.axis_index("y")
    return (x + across) % 4 * 4 + (y + along) % 4, side


def layer_norm(values, gain):
    center = values - jnp.mean(values, axis=-1, keepdims=True)
    spread = jnp.mean(center * center, axis=-1, keepdims=True)
    return center * lax.rsqrt(spread + 1e-05) * gain


def prepare_kernel(
    frames, mask, gain, wq, wk, wv, wo, we, wd, top, bottom, heads, others
):
    normed = layer_norm(frames[...].astype(F32), gain[...].reshape(1, D)).astype(BF16)
    top[...] = normed[:PART]
    bottom[...] = normed[PART:]
    count = jnp.sum(mask[...].astype(F32))
    lane = lax.broadcasted_iota(jnp.int32, (12, 128), 1)
    fill = jnp.where(lane == HD, count, 0.0).astype(BF16)
    heads[...] = jnp.zeros(heads.shape, BF16)
    for m, w in enumerate((wq, wk, wv)):
        for h in range(16):
            part = jnp.concatenate([w[:, h * HD : (h + 1) * HD], fill[:, HD:]], axis=1)
            heads[h, 0:12, m * 128 : (m + 1) * 128] = part
    others[...] = jnp.concatenate([wo[...], we[:, 0:D], we[:, D : 2 * D], wd[...]], axis=0)


def prepare(frames, mask, gain, wq, wk, wv, wo, we, wd):
    return pl.pallas_call(
        prepare_kernel,
        in_specs=[VMEM] * 9,
        out_specs=(VMEM,) * 4,
        out_shape=(
            jax.ShapeDtypeStruct((PART, D), BF16),
            jax.ShapeDtypeStruct((PART, D), BF16),
            jax.ShapeDtypeStruct((16, 16, 384), BF16),
            jax.ShapeDtypeStruct((48, D), BF16),
        ),
        compiler_params=params(56),
        name="prepare",
    )(frames, mask, gain, wq, wk, wv, wo, we, wd)


def project_rows(first, counts, rows, w, q_out, kv_out):
    n = rows.shape[0]
    lane = lax.broadcasted_iota(jnp.int32, (PART, 128), 1)
    row = lax.broadcasted_iota(jnp.int32, (PART, 128), 0)
    product = jnp.dot(rows.reshape(n * PART, D), w, preferred_element_type=F32)
    for j in range(n):
        part = product[j * PART : (j + 1) * PART]
        chunk, side = where_part(first + j)
        bias = jnp.where(row < counts[chunk] - side * PART, 0.0, NEG)
        span = slice((first + j) % 24 * PART, ((first + j) % 24 + 1) * PART)
        q_out[span, :] = jnp.where(lane == HD, 1.0, part[:, 0:128]).astype(BF16)
        kv_out[span, 0:128] = jnp.where(lane == HD, bias, part[:, 128:256]).astype(BF16)
        kv_out[span, 128:256] = jnp.where(lane == HD, 1.0, part[:, 256:384]).astype(BF16)


def early_kernel(counts, *refs):
    pieces, (own_w, other_w, q_out, kv_out, w_out), passed = refs[:6], refs[6:11], refs[11:15]
    rows, held, sems = refs[15:]
    c, z = lax.axis_index("c"), lax.axis_index("z")
    w_copies = [
        pltpu.make_async_copy(own_w, held.at[c], sems.at[6]),
        pltpu.make_async_copy(other_w, held.at[1 - c], sems.at[7]),
    ]
    for copy in w_copies:
        copy.start()
    copies = []
    for p in range(6):
        copies.append(
            pltpu.make_async_copy(pieces[p], rows.at[4 * p : 4 * p + 4], sems.at[p])
        )
        copies[-1].start()
    for copy in w_copies:
        copy.wait()
    for chunk in range(16):
        for core in range(2):
            w_out[(chunk * 2 + core) * 48 : (chunk * 2 + core + 1) * 48, :] = jnp.concatenate(
                [
                    held[core, k ^ z, chunk, 0:12, :]
                    for k in range(4)
                ],
                axis=0,
            )
    onward = []
    for side in range(2):
        for p in range(3):
            copies[side * 3 + p].wait()
        for k, first in ((0, 4), (1, 10)):
            first = first + 12 * side
            onward.append(
                pltpu.make_async_copy(
                    rows.at[first : first + 2], passed[2 * side + k], sems.at[8 + 2 * side + k]
                )
            )
            onward[-1].start()
        project_rows(
            12 * side, counts, rows[12 * side : 12 * side + 12], w_out[...], q_out, kv_out
        )
    for copy in onward:
        copy.wait()


def project_early(counts, pieces, own_w, other_w):
    return pl.pallas_call(
        early_kernel,
        in_specs=[SMEM] + [HBM] * 8,
        out_specs=(VMEM, VMEM, VMEM, HBM, HBM, HBM, HBM),
        out_shape=(
            jax.ShapeDtypeStruct((EARLY, 128), BF16),
            jax.ShapeDtypeStruct((EARLY, 256), BF16),
            jax.ShapeDtypeStruct((D, 384), BF16),
        )
        + (jax.ShapeDtypeStruct((2, PART, D), BF16),) * 4,
        scratch_shapes=[
            pltpu.VMEM((24, PART, D), BF16),
            pltpu.VMEM((2, 4, 16, 16, 384), BF16),
            pltpu.SemaphoreType.DMA((12,)),
        ],
        compiler_params=params(20),
        cost_estimate=pl.CostEstimate(
            flops=EARLY * D * 128, bytes_accessed=2**20, transcendentals=0
        ),
        name="project_early",
    )(counts, *pieces, own_w, other_w)


def late_kernel(counts, p0, p1, p2, p3, w, q_out, kv_out, rows, sems):
    copies = [
        pltpu.make_async_copy(p, rows.at[2 * i : 2 * i + 2], sems.at[i])
        for i, p in enumerate((p0, p1, p2, p3))
    ]
    for copy in copies:
        copy.start()
    for copy in copies:
        copy.wait()
    project_rows(24, counts, rows[...], w[...], q_out, kv_out)


def project_late(counts, pieces, w):
    return pl.pallas_call(
        late_kernel,
        in_specs=[SMEM] + [HBM] * 4 + [VMEM],
        out_specs=(VMEM, VMEM),
        out_shape=(
            jax.ShapeDtypeStruct((LATE, 128), BF16),
            jax.ShapeDtypeStruct((LATE, 256), BF16),
        ),
        scratch_shapes=[pltpu.VMEM((8, PART, D), BF16), pltpu.SemaphoreType.DMA((4,))],
        compiler_params=params(12),
        cost_estimate=pl.CostEstimate(
            flops=2 * LATE * D * 512, bytes_accessed=4 * 2**20, transcendentals=0
        ),
        name="project_late",
    )(counts, *pieces, w)


def largest(rows):
    wide = rows.astype(F32)
    lane = lax.broadcasted_iota(jnp.int32, wide.shape, 1)
    square = jnp.where(lane < HD, wide * wide, 0.0).astype(BF16)
    sums = jnp.dot(square, jnp.ones((128, 128), BF16), preferred_element_type=F32)
    return jnp.max(jnp.max(sums.reshape(-1, 8, 128), axis=0)) * 1.02


def attend_block(q, sources, bounded, first, finish):
    rows = q.shape[0]
    def scores(ref, start):
        return lax.dot_general(
            q,
            ref[pl.ds(start, BK), 0:128],
            (((1,), (1,)), ((), ())),
            preferred_element_type=F32,
        )

    def start_values():
        if first is None:
            return jnp.full((rows, 1), -3e38, F32), jnp.zeros((rows, 128), F32)
        return first()

    @pl.when(bounded)
    def _():
        acc = start_values()[1]
        for ref in sources:
            for i in range(ref.shape[0] // BK):
                p = jnp.exp2(scores(ref, i * BK) * SCALE).astype(BF16)
                acc = acc + jnp.dot(
                    p, ref[pl.ds(i * BK, BK), 128:256], preferred_element_type=F32
                )
        finish(jnp.zeros((rows, 1), F32), acc)

    @pl.when(jnp.logical_not(bounded))
    def _():
        def body(ref, i, carry):
            peak, acc = carry
            start = pl.multiple_of(i * BK, BK)
            s = scores(ref, start) * SCALE
            higher = jnp.maximum(peak, jnp.max(s, axis=1, keepdims=True))
            p = jnp.exp2(s - higher).astype(BF16)
            acc = acc * jnp.exp2(peak - higher) + jnp.dot(
                p, ref[pl.ds(start, BK), 128:256], preferred_element_type=F32
            )
            return higher, acc

        carry = start_values()
        for ref in sources:
            carry = lax.fori_loop(
                0, ref.shape[0] // BK, functools.partial(body, ref), carry
            )
        finish(*carry)


def limit(q, norm):
    return largest(q) * norm <= 60.0 * 60.0 * HD


def attend_early_kernel(q_ref, own, other, o_ref, norm):
    @pl.when(pl.program_id(0) == 0)
    def _():
        norm[0] = jnp.maximum(largest(own[:, 0:128]), largest(other[:, 0:128]))

    def finish(shift, acc):
        lane = lax.broadcasted_iota(jnp.int32, (BQ, 128), 1)
        acc = jnp.where(lane == HD + 1, shift, acc)
        o_ref[...] = jnp.where(lane == HD + 2, norm[0], acc)

    q = q_ref[...]
    attend_block(q, (own, other), limit(q, norm[0]), None, finish)


def attend_early(q, own, other):
    whole = pl.BlockSpec((EARLY, 256), lambda i: (0, 0))
    return pl.pallas_call(
        attend_early_kernel,
        grid=(EARLY // BQ,),
        in_specs=[pl.BlockSpec((BQ, 128), lambda i: (i, 0)), whole, whole],
        out_specs=pl.BlockSpec((BQ, 128), lambda i: (i, 0)),
        out_shape=jax.ShapeDtypeStruct((EARLY, 128), F32),
        scratch_shapes=[pltpu.SMEM((1,), F32)],
        compiler_params=params(28),
        cost_estimate=pl.CostEstimate(
            flops=EARLY * EARLY * 256, bytes_accessed=5 * 2**20, transcendentals=0
        ),
        name="attend_early",
    )(q, own, other)


def attend_late_kernel(
    table, q1, q2, own1, other1, own2, other2, sums, packed, norm, o_ref
):
    block = pl.program_id(0)
    x, y = lax.axis_index("x"), lax.axis_index("y")

    @pl.when(block == 0)
    def _():
        now = jnp.maximum(largest(own2[:, 0:128]), largest(other2[:, 0:128]))
        norm[0] = jnp.maximum(now, jnp.max(sums[0:8, HD + 2 : HD + 3]))

    def finish(shift, acc):
        out = (acc * (1.0 / acc[:, HD : HD + 1])).astype(BF16)
        for t in range(acc.shape[0] // PART):
            part = block * (BQ // PART) + t
            chunk = (x + table[1, part]) % 4 * 4 + (y + table[2, part]) % 4
            spot = pl.multiple_of(chunk * ROWS + table[0, part] * PART, PART)
            o_ref[pl.ds(spot, PART), :] = out[t * PART : (t + 1) * PART]

    @pl.when(block < EARLY // BQ)
    def _():
        q = q1[...]
        shift = sums[:, HD + 1 : HD + 2]
        settled = jnp.max(jnp.abs(shift)) == 0.0
        attend_block(
            q,
            (own2, other2),
            jnp.logical_and(limit(q, norm[0]), settled),
            lambda: (shift, sums[...]),
            finish,
        )

    @pl.when(block == EARLY // BQ)
    def _():
        q = q2[...]
        attend_block(q, (own1, other1, own2, other2), limit(q, norm[0]), None, finish)

        for chunk in range(16):
            rows = o_ref[chunk * ROWS : (chunk + 1) * ROWS, :]
            rest = [rows[FULL:, 32 * i : 32 * i + 32] for i in range(3)]
            packed[chunk] = jnp.concatenate(
                [rows[:FULL, 0:HD], jnp.concatenate(rest, axis=0)], axis=1
            )


def attend_late(q1, q2, own1, other1, own2, other2, sums):
    last = EARLY // BQ - 1

    def whole(rows, width):
        return pl.BlockSpec((rows, width), lambda i: (0, 0))

    def block(width):
        return pl.BlockSpec((BQ, width), lambda i: (jnp.minimum(i, last), 0))

    total = EARLY + LATE
    return pl.pallas_call(
        attend_late_kernel,
        grid=(EARLY // BQ + 1,),
        in_specs=[
            SMEM,
            block(128),
            whole(LATE, 128),
            whole(EARLY, 256),
            whole(EARLY, 256),
            whole(LATE, 256),
            whole(LATE, 256),
            block(128),
        ],
        out_specs=pl.BlockSpec((16, FULL, 128), lambda i: (0, 0, 0)),
        out_shape=jax.ShapeDtypeStruct((16, FULL, 128), BF16),
        scratch_shapes=[pltpu.SMEM((1,), F32), pltpu.VMEM((total, 128), BF16)],
        compiler_params=params(28),
        cost_estimate=pl.CostEstimate(
            flops=8 * (total * total - EARLY * EARLY) * 256,
            bytes_accessed=7 * 2**20,
            transcendentals=0,
        ),
        name="attend_late",
    )(jnp.array(parts(), jnp.int32).T, q1, q2, own1, other1, own2, other2, sums)


def unpack(target, tiles, k):
    low, high = 12 * k, 12 * k + 12
    for s in range(32):
        parts = []
        for i in range(4):
            for t in range(low // 16, (high - 1) // 16 + 1):
                a, b = max(low - 16 * t, 0), min(high - 16 * t, 16)
                parts.append(tiles[t][4 * s + i, a:b, :])
        target[48 * s : 48 * s + 48, :] = jnp.concatenate(parts, axis=0)


def expand_kernel(
    mask,
    att,
    frames,
    gain,
    weights,
    after_out,
    gated_out,
    head_out,
    tail_out,
    rows,
    t0,
    t1,
    t2,
    w,
    w2,
    sems,
):
    tiles = (t0, t1, t2)
    copies = [
        pltpu.make_async_copy(weights.at[:, 16 * t : 16 * t + 16, :], tiles[t], sems.at[t])
        for t in range(3)
    ]
    for copy in copies:
        copy.start()
    for h in range(16):
        rows[0:FULL, h * HD : (h + 1) * HD] = att[h, :, 0:HD]
        for i in range(3):
            cols = slice(h * HD + 32 * i, h * HD + 32 * i + 32)
            rows[FULL:ROWS, cols] = att[h, 48 * i : 48 * i + 48, HD:128]
    copies[0].wait()
    unpack(w, tiles, 0)
    out_term = jnp.dot(rows[...], w[...], preferred_element_type=F32)
    after = frames[...].astype(F32) + out_term
    after_out[...] = after
    normed = layer_norm(after, gain[...].reshape(1, D)).astype(BF16)
    copies[1].wait()
    unpack(w2, tiles, 1)
    copies[2].wait()
    unpack(w, tiles, 2)
    count = jnp.sum(mask[...].astype(F32))
    real = lax.broadcasted_iota(jnp.int32, (ROWS, 1), 0).astype(F32) < count
    for n in range(3):
        cols = slice(n * 512, (n + 1) * 512)
        left = jnp.dot(normed, w2[:, cols], preferred_element_type=F32)
        right = jnp.dot(normed, w[:, cols], preferred_element_type=F32)
        gate = left * (1.0 / (1.0 + jnp.exp(-right)))
        gated = jnp.where(real, gate, 0.0).astype(BF16)
        gated_out[:, cols] = gated
        head_out[:, cols] = gated[0:16]
        tail_out[:, cols] = gated[ROWS - 16 : ROWS]


def expand(mask, att, frames, gain, weights):
    return pl.pallas_call(
        expand_kernel,
        in_specs=[VMEM, VMEM, VMEM, VMEM, HBM],
        out_specs=(VMEM,) * 4,
        out_shape=(
            jax.ShapeDtypeStruct((ROWS, D), F32),
            jax.ShapeDtypeStruct((ROWS, D), BF16),
            jax.ShapeDtypeStruct((16, D), BF16),
            jax.ShapeDtypeStruct((16, D), BF16),
        ),
        scratch_shapes=[pltpu.VMEM((ROWS, D), BF16)]
        + [pltpu.VMEM((128, 16, D), BF16)] * 3
        + [pltpu.VMEM((D, D), BF16)] * 2
        + [pltpu.SemaphoreType.DMA((3,))],
        compiler_params=params(44),
        cost_estimate=pl.CostEstimate(
            flops=2 * ROWS * D * D * 3, bytes_accessed=20 * 2**20, transcendentals=ROWS * D
        ),
        name="expand",
    )(mask, att, frames, gain, weights)


def mix_kernel(gated, taps, mixed, wide):
    wide[0:16, :] = jnp.zeros((16, D), F32)
    wide[16 : 16 + ROWS, :] = gated[...].astype(F32)
    wide[16 + ROWS : 32 + ROWS, :] = jnp.zeros((16, D), F32)
    for n in range(D // 128):
        cols = slice(n * 128, (n + 1) * 128)
        for r in range(0, ROWS, PART):
            acc = jnp.zeros((PART, 128), F32)
            for s in range(8):
                shifted = wide[r + s : r + s + PART + 24, cols]
                for a in range(4):
                    k = 8 * a + s - 1
                    if 0 <= k < KERNEL:
                        acc = acc + shifted[8 * a : 8 * a + PART] * taps[k : k + 1, cols]
            mixed[r : r + PART, cols] = acc


def mix(gated, taps):
    return pl.pallas_call(
        mix_kernel,
        in_specs=[VMEM, VMEM],
        out_specs=VMEM,
        out_shape=jax.ShapeDtypeStruct((ROWS, D), F32),
        scratch_shapes=[pltpu.VMEM((ROWS + 32, D), F32)],
        compiler_params=params(16),
        cost_estimate=pl.CostEstimate(
            flops=2 * ROWS * D * KERNEL * 16, bytes_accessed=14 * 2**20, transcendentals=0
        ),
        name="mix",
    )(gated, taps)


def down_kernel(
    mixed, before, behind, after, taps, gain, weights, out, wide, head, tail, tile, w, sem
):
    copy = pltpu.make_async_copy(weights.at[:, 32:48, :], tile, sem)
    copy.start()
    wide[...] = mixed[...]
    head[0:16, :] = before[...].astype(F32)
    head[16:32, :] = jnp.zeros((16, D), F32)
    tail[0:16, :] = jnp.zeros((16, D), F32)
    tail[16:32, :] = behind[...].astype(F32)
    for n in range(D // 128):
        cols = slice(n * 128, (n + 1) * 128)
        top = wide[0:16, cols]
        for k in range(15):
            top = top + head[k + 1 : k + 17, cols] * taps[k : k + 1, cols]
        wide[0:16, cols] = top
        bottom = wide[ROWS - 16 : ROWS, cols]
        for k in range(16, KERNEL):
            bottom = bottom + tail[k - 15 : k + 1, cols] * taps[k : k + 1, cols]
        wide[ROWS - 16 : ROWS, cols] = bottom
    normed = layer_norm(wide[...], gain[...].reshape(1, D))
    activated = (normed / (1.0 + jnp.exp(-normed))).astype(BF16)
    copy.wait()
    unpack(w, (None, None, tile), 3)
    term = jnp.dot(activated, w[...], preferred_element_type=F32)
    out[...] = (after[...] + term).astype(BF16)


def down(mixed, before, behind, after, taps, gain, weights):
    return pl.pallas_call(
        down_kernel,
        in_specs=[VMEM] * 6 + [HBM],
        out_specs=VMEM,
        out_shape=jax.ShapeDtypeStruct((ROWS, D), BF16),
        scratch_shapes=[
            pltpu.VMEM((ROWS, D), F32),
            pltpu.VMEM((32, D), F32),
            pltpu.VMEM((32, D), F32),
            pltpu.VMEM((128, 16, D), BF16),
            pltpu.VMEM((D, D), BF16),
            pltpu.SemaphoreType.DMA,
        ],
        compiler_params=params(48),
        cost_estimate=pl.CostEstimate(
            flops=2 * ROWS * D * D, bytes_accessed=8 * 2**20, transcendentals=ROWS * D
        ),
        name="down",
    )(mixed, before, behind, after, taps, gain, weights)


def on_device(
    frames,
    frame_mask,
    attend_gain,
    w_query,
    w_key,
    w_value,
    w_out,
    conv_gain,
    w_expand,
    depth_kernel,
    depth_gain,
    w_down,
):
    own_frames = frames[0]

    top, bottom, heads, others = prepare(
        own_frames, frame_mask, attend_gain, w_query, w_key, w_value, w_out, w_expand, w_down
    )

    weights = lax.all_gather(others, ("x", "y", "c", "z"), axis=0)

    line0, line1 = gathered(top, "x"), gathered(bottom, "y")

    heads, *_ = lax.optimization_barrier((heads, line1[1]))
    heads = lax.all_to_all(heads, ("x", "y"), split_axis=0, concat_axis=0, tiled=True)
    counts = heads[:, 0, HD].astype(jnp.int32)
    line0, line1, heads = lax.optimization_barrier((line0, line1, heads))
    early = plane(line0, "y") + plane(line1, "x")
    swap = [[(i, i ^ k) for i in range(4)] for k in (1, 2)]
    own_w = jnp.stack([heads, lax.ppermute(heads, "z", swap[0])])
    own_w = jnp.concatenate([own_w, lax.ppermute(own_w, "z", swap[1])])
    early, own_w = lax.optimization_barrier((early, own_w))
    other_w = pull(own_w, "c", 1)

    q1, kv1, w, *passed = project_early(counts, early, own_w, other_w)
    late = [pull(p, a, j) for p, a, j in zip(passed, ("y", "y", "x", "x"), (1, 3, 1, 3))]
    kv1_other = pull(kv1, "c", 1)
    sums = attend_early(q1, kv1, kv1_other)
    w, sums = lax.optimization_barrier((w, sums))
    q2, kv2 = project_late(counts, late, w)
    kv2_other = pull(kv2, "c", 1)
    attended = attend_late(q1, q2, kv1, kv1_other, kv2, kv2_other, sums)
    attended = lax.all_to_all(attended, ("x", "y"), split_axis=0, concat_axis=0, tiled=True)

    after, gated, head, tail = expand(frame_mask, attended, own_frames, conv_gain, weights)
    line = ("x", "y", "c")
    before = lax.ppermute(tail, line, [(i, i + 1) for i in range(31)])
    behind = lax.ppermute(head, line, [(i + 1, i) for i in range(31)])
    mixed = mix(gated, depth_kernel)
    out = down(mixed, before, behind, after, depth_kernel, depth_gain, weights)
    return out[None]


def solution(mesh):
    cells = Mesh(mesh.devices.reshape(4, 4, 2, 4), ("x", "y", "c", "z"))
    seq = ("x", "y", "c")
    spread = P(("x", "y", "c", "z"), None)
    in_specs = (
        P("z", seq, None),
        P("z", seq),
        P(),
        spread,
        spread,
        spread,
        spread,
        P(),
        spread,
        P(),
        P(),
        spread,
    )
    return jax.shard_map(
        on_device, mesh=cells, in_specs=in_specs, out_specs=P("z", seq, None), check_vma=False
    )
```
